512 devices in a mesh: energy: 32 (over z, core), section: 16 (over y, x).
Axes of the slice: x: 4, y: 4, z: 16, core: 2. Of those that a mesh axis runs over, the one named last changes fastest.
Arguments:
- g_less: float32 [512, 16, 1024], P('energy', 'section'), may hold values from -6 to 6
- g_greater: float32 [512, 16, 1024], P('energy', 'section'), may hold values from -6 to 6
- partner: int32 [16, 1024], P('section'), may hold values from 0 to 1023, each once within a row
- pair_rows: int32 [16, 1024], P('section'), may hold values from 0 to 415
- pair_weight: float32 [16, 1024], P('section'), may hold values from -1.8 to 1.8
- source: float32 [16, 416], P('section'), may hold values from -6 to 6
- slab_inverse: float32 [16, 416, 416], P('section'), may hold values from -0.25 to 1.25
- coupling: float32 [16, 416, 416], P('section'), may hold values from -0.3125 to 0.3125
Outputs:
- sigma: float32 [512, 16, 1024], P(None, 'section', 'energy')
The draws below stay inside these ranges and needn't reach their ends.
Inputs may be any that keep to these rules, and one draw needn't show every extreme that they name: `partner`: each slab's row lists every one of its 1024 pair columns once.
All inputs are finite; a program needn't handle non-finite values.
Results may differ from the reference program's by a relative error of at most 0.0003.
Values sent between devices are 32-bit elements; how exact they have to be, the bound alone decides.
A program may use at most 64 MiB of HBM per device.

```python
import math
import jax
import jax.numpy as jnp
from jax import lax

ORB = 416
NE = 512
NS = 16
NP = 1024


def draw_slab_inverse(key, part):
    key = jax.random.fold_in(key, 7)
    diag_key, off_key = jax.random.split(key)
    diagonal = jnp.exp(jax.random.uniform(diag_key, (NS, ORB), jnp.float32, math.log(0.6), math.log(1.2)))
    offdiag = jax.random.truncated_normal(off_key, -4.0, 4.0, (NS, ORB, ORB), jnp.float32) * (0.3 / ORB ** 0.5)
    left_index = lax.broadcasted_iota(jnp.int32, (ORB, ORB), 0)
    right_index = lax.broadcasted_iota(jnp.int32, (ORB, ORB), 1)
    identity = (left_index == right_index).astype(jnp.float32)
    return offdiag * (1.0 - identity)[None] + identity[None] * diagonal[:, :, None]


def set_ends(array, own_key, least, high):
    place = [jax.random.randint(jax.random.fold_in(own_key, axis), (), 0, length) for axis, length in enumerate(array.shape)]
    main_axis = array.shape.index(max(array.shape))
    next_to = place[:main_axis] + [(place[main_axis] + 1) % array.shape[main_axis]] + place[main_axis + 1:]
    return array.at[tuple(place)].set(least).at[tuple(next_to)].set(high)


def steps_of(rng, extent, cuts, low, top_value):
    def one(dim, parts):
        draws = jax.random.uniform(jax.random.fold_in(jax.random.fold_in(rng, 6), dim), (parts,), jnp.float32, low / len(cuts), top_value / len(cuts))
        return jnp.repeat(jnp.exp(draws), extent[dim] // parts).reshape((-1,) + (1,) * (len(extent) - dim - 1))

    gain = one(*cuts[0])
    for cut in cuts[1:]:
        gain = gain * one(*cut)
    return gain


def scatter_about(rng, dims, deviation, reach, cuts=(), dtype=jnp.bfloat16):
    result = deviation * jax.random.normal(rng, dims, jnp.float32)
    if cuts:
        result = result * steps_of(rng, dims, cuts, -0.22, 0.18)
    return jnp.clip(result, -reach, reach).astype(dtype)


def setup_inputs(seed: int = 0) -> dict:
    keys = jax.random.split(jax.random.key(seed), 9)
    g_less = scatter_about(keys[0], (NE, NS, NP), 1.0, 6.0, ((0, 32), (1, 16)), jnp.float32)
    g_greater = scatter_about(keys[1], (NE, NS, NP), 1.0, 6.0, ((0, 32), (1, 16)), jnp.float32)
    partner = jax.vmap(lambda own: jax.random.permutation(own, NP))(jax.random.split(keys[2], NS)).reshape((NS, NP)).astype(jnp.int32)
    pair_rows = set_ends(jax.random.randint(keys[3], (NS, NP), 0, ORB), jax.random.fold_in(keys[3], 1), 0, ORB - 1).astype(jnp.int32)
    pair_weight = scatter_about(keys[4], (NS, NP), 0.3, 1.8, ((0, 16),), jnp.float32)
    source = scatter_about(keys[5], (NS, ORB), 1.0, 6.0, ((0, 16),), jnp.float32)
    slab_inverse = draw_slab_inverse(jax.random.fold_in(keys[8], 71), 0)
    coupling = scatter_about(keys[7], (NS, ORB, ORB), ORB ** -0.5, 0.3125, ((0, 16),), jnp.float32)
    return dict(g_less=g_less, g_greater=g_greater, partner=partner, pair_rows=pair_rows, pair_weight=pair_weight, source=source, slab_inverse=slab_inverse, coupling=coupling)


highest = lax.Precision.HIGHEST


def correlate(first_seq, second_seq):
    size_count = first_seq.shape[0]
    length = 2 * size_count
    half_count = size_count // 2
    first_spec = jnp.fft.rfft(first_seq, n=length, axis=0)
    second_spec = jnp.fft.rfft(second_seq, n=length, axis=0)
    lagged = jnp.fft.irfft(first_spec * jnp.conj(second_spec), n=length, axis=0)
    return jnp.concatenate([lagged[length - half_count:], lagged[:half_count]], axis=0) * size_count ** -0.5


def convolve(first_seq, second_seq):
    size_count = first_seq.shape[0]
    length = 2 * size_count
    half_count = size_count // 2
    first_spec = jnp.fft.rfft(first_seq, n=length, axis=0)
    second_spec = jnp.fft.rfft(second_seq, n=length, axis=0)
    full_conv = jnp.fft.irfft(first_spec * second_spec, n=length, axis=0)
    return full_conv[half_count:half_count + size_count] * size_count ** -0.5


def reference(g_less, g_greater, partner, pair_rows, pair_weight, source, slab_inverse, coupling):
    energy_count = g_less.shape[0]
    swapped = jnp.take_along_axis(g_greater, jnp.broadcast_to(partner[None], g_greater.shape), axis=2)
    less_slabs = jnp.transpose(g_less, (1, 0, 2))
    swapped_slabs = jnp.transpose(swapped, (1, 0, 2))
    polar = lax.map(lambda pieces: correlate(pieces[0], pieces[1]), (less_slabs, swapped_slabs))
    weighted = polar * pair_weight[:, None, :]
    summed = jax.vmap(lambda values, indices: jax.ops.segment_sum(jnp.transpose(values), indices, num_segments=ORB))(weighted, pair_rows)
    local_pol = jnp.transpose(summed, (2, 0, 1))
    base = jnp.einsum('sij,sj->si', slab_inverse, source, precision=highest)
    guess = base[None] + jnp.einsum('sij,esj->esi', slab_inverse, local_pol * base[None], precision=highest)
    upward = jnp.einsum('sji,esj->esi', coupling, guess, precision=highest)
    upper = jnp.concatenate([upward[:, 1:], jnp.zeros_like(upward[:, :1])], axis=1)
    rhs = source[None] + local_pol * guess + upper

    def advance(carried, slab_data):
        inverse_block, couple_block, right_side = slab_data
        inner = right_side + jnp.einsum('ij,ej->ei', couple_block, carried, precision=highest)
        fresh = jnp.einsum('ij,ej->ei', inverse_block, inner, precision=highest)
        return fresh, fresh

    start_value = jnp.zeros((energy_count, ORB), jnp.float32)
    final_value, screened = lax.scan(advance, start_value, (slab_inverse, coupling, jnp.transpose(rhs, (1, 0, 2))))
    row_index = jnp.broadcast_to(pair_rows[:, None, :], (NS, energy_count, NP))
    pair_values = jnp.take_along_axis(screened, row_index, axis=2) * pair_weight[:, None, :]
    sigma_slabs = lax.map(lambda pieces: convolve(pieces[0], pieces[1]), (less_slabs, pair_values))
    return jnp.transpose(sigma_slabs, (1, 0, 2))
```

```python
import functools
import math

import jax
import jax.numpy as jnp
import numpy as np
from jax import lax
from jax.experimental import pallas as pl
from jax.experimental.pallas import tpu as pltpu
from jax.sharding import PartitionSpec as P

MESH = pl.DeviceIdType.MESH
F32 = jnp.float32
BF16 = jnp.bfloat16
NT = (((1,), (1,)), ((), ()))
NN = (((1,), (0,)), ((), ()))
LENGTH = 768
HALF = LENGTH // 2


def two_parts(table):
    table = np.asarray(table, np.float32)
    high = table.astype(jnp.bfloat16)
    low = (table - high.astype(np.float32)).astype(jnp.bfloat16)
    return jnp.asarray(high), jnp.asarray(low)


def angles(times):
    return np.outer(np.arange(HALF) + 0.5, np.asarray(times, np.float64)) * (2.0 * math.pi / LENGTH)


def forward_table(order):
    phase = angles(order)
    return two_parts(np.concatenate([np.cos(phase), np.sin(phase)], axis=0))


def inverse_table(times, energies):
    phase = angles(times).T
    scale = 2.0 / LENGTH / math.sqrt(energies)
    return two_parts(np.concatenate([np.cos(phase), np.sin(phase)], axis=1) * scale)


def energy_order(peers, own, fold):
    rows = own // fold
    group, sender, row = np.meshgrid(np.arange(fold), np.arange(peers), np.arange(rows), indexing="ij")
    return (sender * own + group * rows + row).reshape(-1)


def lanes_of(shape):
    return lax.broadcasted_iota(jnp.int32, shape, len(shape) - 1)


def roll(x, shift, axis=1):
    return pltpu.roll(x, shift, axis)


def exchange_groups(parts):
    a0, a1, a2, a3 = parts
    lane = lanes_of(a0.shape)
    low = lane < 64
    near = lane % 64 < 32
    b0, b2 = jnp.where(low, a0, roll(a2, 64)), jnp.where(low, roll(a0, 64), a2)
    b1, b3 = jnp.where(low, a1, roll(a3, 64)), jnp.where(low, roll(a1, 64), a3)
    c0, c1 = jnp.where(near, b0, roll(b1, 32)), jnp.where(near, roll(b0, 96), b1)
    c2, c3 = jnp.where(near, b2, roll(b3, 32)), jnp.where(near, roll(b2, 96), b3)
    return c0, c1, c2, c3


def exchange_rows(first, second):
    lane = lanes_of(first.shape)
    row = lax.broadcasted_iota(jnp.int32, first.shape, 0)
    low = lane < 64
    upper_half = row < 4
    keep = (lane % 64 < 32) == upper_half
    one, two = jnp.where(low, first, roll(second, 64)), jnp.where(low, roll(first, 64), second)

    def inside(x):
        turned = roll(x, 4, 0)
        return jnp.where(keep, x, jnp.where(upper_half, roll(turned, 32), roll(turned, 96)))

    return inside(one), inside(two)


def split(x):
    high = x.astype(BF16)
    return high, (x - high.astype(F32)).astype(BF16)


def dot(x, y, dims=NN):
    return lax.dot_general(x, y, dims, preferred_element_type=F32)


def product(x, high, low, dims):
    rows = x.shape[0]
    x_high, x_low = split(x)
    both = dot(jnp.concatenate([x_high, x_low], axis=0), high, dims)
    return both[:rows] + both[rows:] + dot(x_high, low, dims)


def scatter_start(peers, me, source, target, send, recv):
    def one(k, _):
        peer = lax.rem(me + k, peers)
        pltpu.make_async_remote_copy(
            src_ref=source.at[peer],
            dst_ref=target.at[me],
            send_sem=send.at[k],
            recv_sem=recv.at[k],
            device_id={"energy": peer},
            device_id_type=MESH,
        ).start()
        return 0

    lax.fori_loop(1, peers, one, 0)
    target[me] = source[me]


def scatter_wait(peers, me, source, target, send, recv):
    def one(k, _):
        peer = lax.rem(me + k, peers)
        copy = pltpu.make_async_remote_copy(
            src_ref=source.at[peer],
            dst_ref=target.at[me],
            send_sem=send.at[k],
            recv_sem=recv.at[k],
            device_id={"energy": peer},
            device_id_type=MESH,
        )
        copy.wait_send()
        copy.wait_recv()
        return 0

    lax.fori_loop(1, peers, one, 0)


def lane_take(x, index):
    return jnp.take_along_axis(x, index, axis=1, mode="promise_in_bounds")


def main_kernel(
    peers, sections,
    less_ref, great_ref, partner_ref, rows_ref, weight_ref, source_ref, inverse_ref, coupling_ref,
    fwd_high, fwd_low, inv_high, inv_low,
    values_out, spectrum_out,
    swapped, first_send, first_recv, second_send, second_recv, third_send,
    tables, table_sem, orbital_table, slab_high, slab_low, couple_high, couple_low, map_high, map_low,
    upward, upper, carried_out, carried_in,
    send_one, recv_one, send_two, recv_two, send_three, recv_three, shift_sem, sweep_sem,
):
    me = lax.axis_index("energy")
    section = lax.axis_index("section")
    has_before = section > 0
    has_after = section < sections - 1
    before = lax.rem(section + sections - 1, sections)
    after = lax.rem(section + 1, sections)
    orbitals = inverse_ref.shape[0]

    barrier = pltpu.get_barrier_semaphore()

    def greet(k, _):
        pl.semaphore_signal(barrier, inc=1, device_id={"energy": lax.rem(me + k, peers)}, device_id_type=MESH)
        return 0

    lax.fori_loop(1, peers, greet, 0)

    @pl.when(has_before)
    def _():
        pl.semaphore_signal(barrier, inc=1, device_id={"section": before}, device_id_type=MESH)

    @pl.when(has_after)
    def _():
        pl.semaphore_signal(barrier, inc=1, device_id={"section": after}, device_id_type=MESH)

    loads = [
        pltpu.make_async_copy(ref, tables.at[place], table_sem.at[place])
        for place, ref in enumerate((fwd_high, fwd_low))
    ]
    for load in loads:
        load.start()

    partner = partner_ref[...]
    partner_tile, partner_lane = partner // 128, partner % 128
    for energy in range(16):
        total = jnp.zeros((8, 128), F32)
        for tile in range(8):
            line = jnp.broadcast_to(great_ref[8 * energy + tile : 8 * energy + tile + 1, :], (8, 128))
            total = jnp.where(partner_tile == tile, lane_take(line, partner_lane), total)
        swapped[8 * energy : 8 * energy + 8, :] = total

    for tile in range(8):
        parts = []
        for h in range(2):
            for ref in (less_ref, swapped):
                parts.append(ref[pl.ds(64 * h + tile, 8, stride=8), :])
        for b, part in enumerate(exchange_groups(parts)):
            first_send[4 * tile + b] = part

    pl.semaphore_wait(barrier, peers - 1 + has_before.astype(jnp.int32) + has_after.astype(jnp.int32))
    scatter_start(peers, me, first_send, first_recv, send_one, recv_one)

    pair_rows = rows_ref[...]
    for tile in range(8):
        index = lax.broadcasted_iota(jnp.int32, (orbitals, 128), 0)
        orbital_table[:, 128 * tile : 128 * tile + 128] = (
            (index == pair_rows[tile : tile + 1, :]).astype(F32).astype(BF16)
        )
    slab_high[...], slab_low[...] = split(inverse_ref[...])
    couple_high[...], couple_low[...] = split(coupling_ref[...])
    slab_map = (
        dot(slab_high[...], couple_high[...])
        + dot(slab_high[...], couple_low[...])
        + dot(slab_low[...], couple_high[...])
    )
    map_high[...], map_low[...] = split(slab_map)
    source = source_ref[...]
    base = product(jnp.broadcast_to(source, (16, orbitals)), slab_high[...], slab_low[...], NT)

    for load in loads:
        load.wait()
    scatter_wait(peers, me, first_send, first_recv, send_one, recv_one)

    blocks = first_recv[...].reshape(peers * 8, 128)
    low_lanes = lanes_of(blocks.shape) < 64
    high = blocks.astype(BF16).astype(F32)
    low = blocks - high
    stacked = jnp.concatenate(
        [
            jnp.where(low_lanes, high, roll(low, 64)).astype(BF16),
            jnp.where(low_lanes, roll(high, 64), low).astype(BF16),
        ],
        axis=0,
    )
    halves = dot(tables[0], stacked) + dot(tables[1], stacked)
    spectrum = halves + roll(halves, 64)
    spectrum_out[...] = spectrum
    other = roll(spectrum, 96)
    cos_a, sin_a, cos_b, sin_b = spectrum[:HALF], spectrum[HALF:], other[:HALF], other[HALF:]
    crossed = jnp.concatenate([cos_a * cos_b + sin_a * sin_b, sin_a * cos_b - cos_a * sin_b], axis=0)
    high = crossed.astype(BF16).astype(F32)
    packed = jnp.where(lanes_of(crossed.shape) < 32, high, roll(crossed - high, 32)).astype(BF16)
    halves = dot(inv_high[...], packed) + dot(inv_low[...], packed)
    polar = halves + roll(halves, 96)
    count = polar.shape[0] // 4
    group = lanes_of((count, 128)) // 32
    joined = polar[:count]
    for q in range(1, 4):
        joined = jnp.where(group == q, roll(polar[count * q : count * (q + 1)], 32 * q), joined)
    second_send[...] = joined.reshape(peers, 4, 128)
    scatter_start(peers, me, second_send, second_recv, send_two, recv_two)
    scatter_wait(peers, me, second_send, second_recv, send_two, recv_two)

    weighted = []
    for tile in range(8):
        lines = [second_recv[4 * tile + b] for b in range(4)]
        one, two = exchange_rows(jnp.concatenate(lines[:2], axis=0), jnp.concatenate(lines[2:], axis=0))
        weighted.append(jnp.concatenate([one, two], axis=0) * weight_ref[tile : tile + 1, :])
    both = dot(jnp.concatenate(split(jnp.concatenate(weighted, axis=1)), axis=0), orbital_table[...], NT)
    local_pol = both[:16] + both[16:]
    guess = base + product(local_pol * base, slab_high[...], slab_low[...], NT)
    upward[...] = product(guess, couple_high[...], couple_low[...], NN)

    upper[...] = jnp.zeros_like(upper)
    shift = pltpu.make_async_remote_copy(
        src_ref=upward,
        dst_ref=carried_in.at[0],
        send_sem=shift_sem.at[0],
        recv_sem=shift_sem.at[1],
        device_id={"section": before},
        device_id_type=MESH,
    )
    sweep = pltpu.make_async_remote_copy(
        src_ref=carried_out,
        dst_ref=carried_in.at[1],
        send_sem=sweep_sem.at[0],
        recv_sem=sweep_sem.at[1],
        device_id={"section": after},
        device_id_type=MESH,
    )

    @pl.when(has_before)
    def _():
        shift.start()

    partial = source + local_pol * guess

    @pl.when(has_after)
    def _():
        shift.wait_recv()
        upper[...] = carried_in[0]

    offset = product(partial + upper[...], slab_high[...], slab_low[...], NT)
    carried_out[...] = offset

    @pl.when(has_before)
    def _():
        sweep.wait_recv()
        carried_out[...] = offset + product(carried_in[1], map_high[...], map_low[...], NT)

    @pl.when(has_after)
    def _():
        sweep.start()

    screened = carried_out[...]
    both = dot(jnp.concatenate(split(screened), axis=0), orbital_table[...])
    pairs = both[:16] + both[16:]
    for tile in range(8):
        piece = pairs[:, 128 * tile : 128 * tile + 128] * weight_ref[tile : tile + 1, :]
        one, two = exchange_rows(piece[:8], piece[8:])
        for b, block in enumerate((one[:4], one[4:], two[:4], two[4:])):
            third_send[4 * tile + b] = block
    scatter_start(peers, me, third_send, values_out, send_three, recv_three)

    @pl.when(has_before)
    def _():
        shift.wait_send()

    @pl.when(has_after)
    def _():
        sweep.wait_send()

    scatter_wait(peers, me, third_send, values_out, send_three, recv_three)


def last_kernel(values_ref, spectrum_ref, fwd_high, fwd_low, inv_high, inv_low, sigma_ref):
    values = values_ref[...].reshape(values_ref.shape[0] * 4, 128)
    lane = lanes_of(values.shape)
    high = values.astype(BF16).astype(F32)
    low = values - high
    stacked = []
    for q in range(4):
        left = high if q == 0 else roll(high, 128 - 32 * q)
        right = roll(low, (160 - 32 * q) % 128) if q != 1 else low
        stacked.append(jnp.where(lane < 32, left, right).astype(BF16))
    stacked = jnp.concatenate(stacked, axis=0)
    halves = dot(fwd_high[...], stacked) + dot(fwd_low[...], stacked)
    wave = halves + roll(halves, 96)
    spectrum = spectrum_ref[...]
    cos_a, sin_a, cos_w, sin_w = spectrum[:HALF], spectrum[HALF:], wave[:HALF], wave[HALF:]
    crossed = jnp.concatenate([cos_a * cos_w - sin_a * sin_w, cos_a * sin_w + sin_a * cos_w], axis=0)
    high = crossed.astype(BF16).astype(F32)
    packed = jnp.where(lanes_of(crossed.shape) < 32, high, roll(crossed - high, 32)).astype(BF16)
    halves = dot(inv_high[...], packed) + dot(inv_low[...], packed)
    full = halves + roll(halves, 96)
    sigma_ref[...] = jnp.transpose(full)[:32]


def on_device(peers, sections, g_less, g_greater, partner, pair_rows, pair_weight, source, slab_inverse, coupling):
    own, _, columns = g_less.shape
    energies = own * peers
    orbitals = slab_inverse.shape[-1]
    polar_times = energy_order(peers, own, 4) - energies // 2
    sigma_times = np.arange(energies) + energies // 2
    vmem = pl.BlockSpec(memory_space=pltpu.VMEM)
    hbm = pl.BlockSpec(memory_space=pl.ANY)
    square = (orbitals, orbitals)
    strip = (own, orbitals)
    values, spectrum = pl.pallas_call(
        functools.partial(main_kernel, peers, sections),
        out_shape=(
            jax.ShapeDtypeStruct((peers, 4, 128), F32),
            jax.ShapeDtypeStruct((LENGTH, 128), F32),
        ),
        in_specs=[vmem] * 8 + [hbm] * 2 + [vmem] * 2,
        out_specs=(vmem, vmem),
        scratch_shapes=[
            pltpu.VMEM((128, 128), F32),
            pltpu.VMEM((peers, 8, 128), F32),
            pltpu.VMEM((peers, 8, 128), F32),
            pltpu.VMEM((peers, 4, 128), F32),
            pltpu.VMEM((peers, 4, 128), F32),
            pltpu.VMEM((peers, 4, 128), F32),
            pltpu.VMEM((2, LENGTH, energies), BF16),
            pltpu.SemaphoreType.DMA((2,)),
            pltpu.VMEM((orbitals, columns), BF16),
            pltpu.VMEM(square, BF16),
            pltpu.VMEM(square, BF16),
            pltpu.VMEM(square, BF16),
            pltpu.VMEM(square, BF16),
            pltpu.VMEM(square, BF16),
            pltpu.VMEM(square, BF16),
            pltpu.VMEM(strip, F32),
            pltpu.VMEM(strip, F32),
            pltpu.VMEM(strip, F32),
            pltpu.VMEM((2,) + strip, F32),
            pltpu.SemaphoreType.DMA((peers,)),
            pltpu.SemaphoreType.DMA((peers,)),
            pltpu.SemaphoreType.DMA((peers,)),
            pltpu.SemaphoreType.DMA((peers,)),
            pltpu.SemaphoreType.DMA((peers,)),
            pltpu.SemaphoreType.DMA((peers,)),
            pltpu.SemaphoreType.DMA((2,)),
            pltpu.SemaphoreType.DMA((2,)),
        ],
        compiler_params=pltpu.CompilerParams(
            collective_id=0, has_side_effects=True, vmem_limit_bytes=32 * 1024 * 1024
        ),
        name="update",
    )(
        g_less.reshape(-1, 128),
        g_greater.reshape(-1, 128),
        partner.reshape(-1, 128),
        pair_rows.reshape(-1, 128),
        pair_weight.reshape(-1, 128),
        source,
        slab_inverse[0],
        coupling[0],
        *forward_table(energy_order(peers, own, 2)),
        *inverse_table(polar_times, energies),
    )
    sigma = pl.pallas_call(
        last_kernel,
        out_shape=jax.ShapeDtypeStruct((columns // peers, energies), F32),
        in_specs=[vmem] * 6,
        out_specs=vmem,
        compiler_params=pltpu.CompilerParams(vmem_limit_bytes=32 * 1024 * 1024),
        name="convolution",
    )(
        values,
        spectrum,
        *forward_table(energy_order(peers, own, 4)),
        *inverse_table(sigma_times, energies),
    )
    return jnp.transpose(sigma)[:, None, :]


def solution(mesh):
    return jax.shard_map(
        functools.partial(on_device, mesh.shape["energy"], mesh.shape["section"]),
        mesh=mesh,
        in_specs=(
            P("energy", "section", None),
            P("energy", "section", None),
            P("section", None),
            P("section", None),
            P("section", None),
            P("section", None),
            P("section", None, None),
            P("section", None, None),
        ),
        out_specs=P(None, "section", "energy"),
        check_vma=False,
    )
```

```python
import functools
import math

import jax
import jax.numpy as jnp
import numpy as np
from jax import lax
from jax.experimental import pallas as pl
from jax.experimental.pallas import tpu as pltpu
from jax.sharding import PartitionSpec as P

MESH = pl.DeviceIdType.MESH
F32 = jnp.float32
BF16 = jnp.bfloat16
NT = (((1,), (1,)), ((), ()))
NN = (((1,), (0,)), ((), ()))
LENGTH = 768
HALF = LENGTH // 2
REACH = 4


def two_parts(table):
    table = np.asarray(table, np.float32)
    high = table.astype(jnp.bfloat16)
    low = (table - high.astype(np.float32)).astype(jnp.bfloat16)
    return jnp.asarray(high), jnp.asarray(low)


def angles(times):
    return np.outer(np.arange(HALF) + 0.5, np.asarray(times, np.float64)) * (2.0 * math.pi / LENGTH)


def forward_table(order):
    phase = angles(order)
    return two_parts(np.concatenate([np.cos(phase), np.sin(phase)], axis=0))


def inverse_table(times, energies):
    phase = angles(times).T
    scale = 2.0 / LENGTH / math.sqrt(energies)
    return two_parts(np.concatenate([np.cos(phase), np.sin(phase)], axis=1) * scale)


def energy_order(peers, own, fold):
    rows = own // fold
    group, sender, row = np.meshgrid(np.arange(fold), np.arange(peers), np.arange(rows), indexing="ij")
    return (sender * own + group * rows + row).reshape(-1)


def lanes_of(shape):
    return lax.broadcasted_iota(jnp.int32, shape, len(shape) - 1)


def roll(x, shift, axis=1):
    return pltpu.roll(x, shift, axis)


def exchange_groups(parts):
    a0, a1, a2, a3 = parts
    lane = lanes_of(a0.shape)
    low = lane < 64
    near = lane % 64 < 32
    b0, b2 = jnp.where(low, a0, roll(a2, 64)), jnp.where(low, roll(a0, 64), a2)
    b1, b3 = jnp.where(low, a1, roll(a3, 64)), jnp.where(low, roll(a1, 64), a3)
    c0, c1 = jnp.where(near, b0, roll(b1, 32)), jnp.where(near, roll(b0, 96), b1)
    c2, c3 = jnp.where(near, b2, roll(b3, 32)), jnp.where(near, roll(b2, 96), b3)
    return c0, c1, c2, c3


def exchange_rows(first, second):
    lane = lanes_of(first.shape)
    row = lax.broadcasted_iota(jnp.int32, first.shape, 0)
    low = lane < 64
    upper_half = row < 4
    keep = (lane % 64 < 32) == upper_half
    one, two = jnp.where(low, first, roll(second, 64)), jnp.where(low, roll(first, 64), second)

    def inside(x):
        turned = roll(x, 4, 0)
        return jnp.where(keep, x, jnp.where(upper_half, roll(turned, 32), roll(turned, 96)))

    return inside(one), inside(two)


def split(x):
    high = x.astype(BF16)
    return high, (x - high.astype(F32)).astype(BF16)


def dot(x, y, dims=NN):
    return lax.dot_general(x, y, dims, preferred_element_type=F32)


def product(x, high, low, dims):
    rows = x.shape[0]
    x_high, x_low = split(x)
    both = dot(jnp.concatenate([x_high, x_low], axis=0), high, dims)
    return both[:rows] + both[rows:] + dot(x_high, low, dims)


def scatter_start(peers, me, source, target, send, recv):
    def one(n, _):
        away = peers // 2 + (n + 1) // 2 * (1 - n % 2 * 2)
        peer = lax.rem(me + away, peers)
        pltpu.make_async_remote_copy(
            src_ref=source.at[peer],
            dst_ref=target.at[me],
            send_sem=send,
            recv_sem=recv,
            device_id={"energy": peer},
            device_id_type=MESH,
        ).start()
        return 0

    lax.fori_loop(0, peers - 1, one, 0)
    target[me] = source[me]


def wait_blocks(peers, ref, semaphore):
    part = ref.at[pl.ds(0, peers - 1)]
    pltpu.make_async_copy(part, part, semaphore).wait()


def lane_take(x, index):
    return jnp.take_along_axis(x, index, axis=1, mode="promise_in_bounds")


def main_kernel(
    peers, sections,
    less_hbm, great_hbm, partner_hbm, rows_hbm, weight_hbm, source_hbm, inverse_hbm, coupling_hbm,
    fwd_high_hbm, fwd_low_hbm, inv_high_hbm, inv_low_hbm,
    values_out, spectrum_out,
    less_ref, great_ref, partner_ref, rows_ref, weight_ref, source_ref, inverse_ref, coupling_ref,
    fwd_high, fwd_low, inv_high, inv_low, load_sem,
    swapped, first_send, first_recv, second_send, second_recv, third_send,
    orbital_table, slab_high, slab_low, couple_high, couple_low,
    steps, inbox, step_high, step_low, next_send, next_recv, twin_send, twin_recv,
    upward, offset, carried, arrived, across_send, across_recv,
    send_one, recv_one, send_two, recv_two, send_three, recv_three,
):
    me = lax.axis_index("energy")
    section = lax.axis_index("section")
    has_before = section > 0
    has_after = section < sections - 1
    after = lax.rem(section + 1, sections)
    orbitals = inverse_ref.shape[0]
    half, first_rows = orbitals // 2, orbitals // 64 * 16 + 16
    core = lax.rem(me, 2)
    twin = me + 1 - 2 * core

    loads = [
        pltpu.make_async_copy(source, target, load_sem.at[place])
        for place, (source, target) in enumerate((
            (great_hbm, great_ref), (partner_hbm, partner_ref), (less_hbm, less_ref), (rows_hbm, rows_ref),
            (weight_hbm, weight_ref), (source_hbm, source_ref), (inverse_hbm, inverse_ref),
            (coupling_hbm, coupling_ref), (fwd_high_hbm, fwd_high), (fwd_low_hbm, fwd_low),
            (inv_high_hbm, inv_high), (inv_low_hbm, inv_low),
        ))
    ]
    for load in loads:
        load.start()

    barrier = pltpu.get_barrier_semaphore()

    def greet(k, _):
        pl.semaphore_signal(barrier, inc=1, device_id={"energy": lax.rem(me + k, peers)}, device_id_type=MESH)
        return 0

    lax.fori_loop(1, peers, greet, 0)

    for away in range(1, REACH + 1):
        for there, other in ((section >= away, section - away), (section < sections - away, section + away)):

            @pl.when(there)
            def _(other=other):
                pl.semaphore_signal(barrier, inc=1, device_id={"section": other}, device_id_type=MESH)

    loads[0].wait()
    loads[1].wait()
    loads[2].wait()

    partner = partner_ref[...]
    partner_tile, partner_lane = partner // 128, partner % 128
    for energy in range(16):
        total = jnp.zeros((8, 128), F32)
        for tile in range(8):
            line = jnp.broadcast_to(great_ref[8 * energy + tile : 8 * energy + tile + 1, :], (8, 128))
            total = jnp.where(partner_tile == tile, lane_take(line, partner_lane), total)
        swapped[8 * energy : 8 * energy + 8, :] = total

    for tile in range(8):
        parts = []
        for h in range(2):
            for ref in (less_ref, swapped):
                parts.append(ref[pl.ds(64 * h + tile, 8, stride=8), :])
        for b, part in enumerate(exchange_groups(parts)):
            first_send[4 * tile + b] = part

    pl.semaphore_wait(barrier, peers - 1 + jnp.minimum(section, REACH) + jnp.minimum(sections - 1 - section, REACH))
    scatter_start(peers, me, first_send, first_recv, send_one, recv_one)

    def rows_of(chunk):
        return pl.ds(0, first_rows) if chunk == 0 else pl.ds(first_rows, half - first_rows)

    def to_next(k, chunk):
        return pltpu.make_async_remote_copy(
            src_ref=steps.at[k - 1, core, rows_of(chunk)],
            dst_ref=inbox.at[k - 1, rows_of(chunk)],
            send_sem=next_send.at[k - 1, chunk],
            recv_sem=next_recv.at[k - 1, chunk],
            device_id={"section": after},
            device_id_type=MESH,
        )

    def to_twin(k, chunk):
        return pltpu.make_async_remote_copy(
            src_ref=steps.at[k - 1, core, rows_of(chunk)],
            dst_ref=steps.at[k - 1, core, rows_of(chunk)],
            send_sem=twin_send.at[k - 1, chunk],
            recv_sem=twin_recv.at[k - 1, chunk],
            device_id={"energy": twin},
            device_id_type=MESH,
        )

    def pass_on(k, chunk):
        @pl.when(has_after)
        def _():
            to_next(k, chunk).start()

    def grow(k, chunk):
        @pl.when(has_before)
        def _():
            to_next(k - 1, chunk).wait_recv()

        rows = rows_of(chunk)
        high, low = split(inbox[k - 2, rows])
        whole_high, whole_low = step_high[0], step_low[0]
        steps[k - 1, core, rows] = dot(high, whole_high) + dot(low, whole_high) + dot(high, whole_low)
        if k < REACH:
            pass_on(k, chunk)
        to_twin(k, chunk).start()

    def gather(k):
        for chunk in range(2):
            to_twin(k, chunk).wait_recv()
        for part in range(2):
            rows = pl.ds(half * part, half)
            step_high[k - 1, rows], step_low[k - 1, rows] = split(steps[k - 1, part])

    @pl.when(jnp.logical_not(has_before))
    def _():
        inbox[...] = jnp.zeros_like(inbox)

    for load in loads[3:8]:
        load.wait()
    slab_high[...], slab_low[...] = split(inverse_ref[...])
    couple_high[...], couple_low[...] = split(coupling_ref[...])
    slab_map = (
        dot(slab_high[...], couple_high[...])
        + dot(slab_high[...], couple_low[...])
        + dot(slab_low[...], couple_high[...])
    )
    map_high, map_low = split(slab_map)
    index = lax.broadcasted_iota(jnp.int32, (orbitals, orbitals), 0)
    identity = (index == lanes_of((orbitals, orbitals))).astype(F32).astype(BF16)
    turned_high, turned_low = dot(identity, map_high, NT), dot(identity, map_low, NT)
    step_high[0], step_low[0] = turned_high.astype(BF16), turned_low.astype(BF16)
    turned = turned_high + turned_low
    steps[0, 0], steps[0, 1] = turned[:half], turned[half:]
    for chunk in range(2):
        pass_on(1, chunk)

    pair_rows = rows_ref[...]
    for tile in range(8):
        index = lax.broadcasted_iota(jnp.int32, (orbitals, 128), 0)
        orbital_table[:, 128 * tile : 128 * tile + 128] = (
            (index == pair_rows[tile : tile + 1, :]).astype(F32).astype(BF16)
        )
    source = source_ref[...]
    base = product(jnp.broadcast_to(source, (16, orbitals)), slab_high[...], slab_low[...], NT)
    grow(2, 0)

    for load in loads[8:]:
        load.wait()
    wait_blocks(peers, first_recv, recv_one)

    blocks = first_recv[...].reshape(peers * 8, 128)
    low_lanes = lanes_of(blocks.shape) < 64
    high = blocks.astype(BF16).astype(F32)
    low = blocks - high
    stacked = jnp.concatenate(
        [
            jnp.where(low_lanes, high, roll(low, 64)).astype(BF16),
            jnp.where(low_lanes, roll(high, 64), low).astype(BF16),
        ],
        axis=0,
    )
    halves = dot(fwd_high[...], stacked) + dot(fwd_low[...], stacked)
    spectrum = halves + roll(halves, 64)
    spectrum_out[...] = spectrum
    other = roll(spectrum, 96)
    cos_a, sin_a, cos_b, sin_b = spectrum[:HALF], spectrum[HALF:], other[:HALF], other[HALF:]
    crossed = jnp.concatenate([cos_a * cos_b + sin_a * sin_b, sin_a * cos_b - cos_a * sin_b], axis=0)
    high = crossed.astype(BF16).astype(F32)
    packed = jnp.where(lanes_of(crossed.shape) < 32, high, roll(crossed - high, 32)).astype(BF16)
    halves = dot(inv_high[...], packed) + dot(inv_low[...], packed)
    polar = halves + roll(halves, 96)
    count = polar.shape[0] // 4
    group = lanes_of((count, 128)) // 32
    joined = polar[:count]
    for q in range(1, 4):
        joined = jnp.where(group == q, roll(polar[count * q : count * (q + 1)], 32 * q), joined)
    second_send[...] = joined.reshape(peers, 4, 128)
    scatter_start(peers, me, second_send, second_recv, send_two, recv_two)
    grow(2, 1)
    grow(3, 0)
    gather(2)
    wait_blocks(peers, second_recv, recv_two)

    weighted = []
    for tile in range(8):
        lines = [second_recv[4 * tile + b] for b in range(4)]
        one, two = exchange_rows(jnp.concatenate(lines[:2], axis=0), jnp.concatenate(lines[2:], axis=0))
        weighted.append(jnp.concatenate([one, two], axis=0) * weight_ref[tile : tile + 1, :])
    both = dot(jnp.concatenate(split(jnp.concatenate(weighted, axis=1)), axis=0), orbital_table[...], NT)
    local_pol = both[:16] + both[16:]
    guess = base + product(local_pol * base, slab_high[...], slab_low[...], NT)
    upward[...] = product(guess, couple_high[...], couple_low[...], NN)

    def across(source, place, away):
        return pltpu.make_async_remote_copy(
            src_ref=source,
            dst_ref=arrived.at[place],
            send_sem=across_send.at[place],
            recv_sem=across_recv.at[place],
            device_id={"section": lax.rem(section + sections + away, sections)},
            device_id_type=MESH,
        )

    shift = across(upward, 0, -1)
    window = [across(offset, away, away) for away in range(1, REACH)]
    sweep = across(carried, REACH, REACH)

    @pl.when(has_before)
    def _():
        shift.start()

    grow(3, 1)
    partial = source + local_pol * guess

    @pl.when(has_after)
    def _():
        shift.wait_recv()

    @pl.when(jnp.logical_not(has_after))
    def _():
        arrived[0] = jnp.zeros_like(upward)

    offset[...] = product(partial + arrived[0], slab_high[...], slab_low[...], NT)
    for away in range(1, REACH):

        @pl.when(section < sections - away)
        def _(away=away):
            window[away - 1].start()

    gather(3)
    grow(4, 0)
    carried[...] = offset[...]
    for away in range(1, REACH):

        @pl.when(section >= away)
        def _(away=away):
            window[away - 1].wait_recv()
            carried[...] += product(arrived[away], step_high[away - 1], step_low[away - 1], NN)

    @pl.when(section < REACH)
    def _():
        sweep.start()

    grow(4, 1)
    gather(4)

    @pl.when(section >= REACH)
    def _():
        sweep.wait_recv()
        carried[...] += product(arrived[REACH], step_high[REACH - 1], step_low[REACH - 1], NN)

        @pl.when(section < sections - REACH)
        def _():
            sweep.start()

    screened = carried[...]
    both = dot(jnp.concatenate(split(screened), axis=0), orbital_table[...])
    pairs = both[:16] + both[16:]
    for tile in range(8):
        piece = pairs[:, 128 * tile : 128 * tile + 128] * weight_ref[tile : tile + 1, :]
        one, two = exchange_rows(piece[:8], piece[8:])
        for b, block in enumerate((one[:4], one[4:], two[:4], two[4:])):
            third_send[4 * tile + b] = block
    scatter_start(peers, me, third_send, values_out, send_three, recv_three)

    @pl.when(has_before)
    def _():
        shift.wait_send()

    for away in range(1, REACH):

        @pl.when(section < sections - away)
        def _(away=away):
            window[away - 1].wait_send()

    @pl.when(section < sections - REACH)
    def _():
        sweep.wait_send()

    for chunk in range(2):

        @pl.when(has_after)
        def _(chunk=chunk):
            for k in range(1, REACH):
                to_next(k, chunk).wait_send()

        for k in range(2, REACH + 1):
            to_twin(k, chunk).wait_send()

    wait_blocks(peers, first_send, send_one)
    wait_blocks(peers, second_send, send_two)
    wait_blocks(peers, third_send, send_three)
    wait_blocks(peers, values_out, recv_three)


def last_kernel(values_ref, spectrum_ref, fwd_high, fwd_low, inv_high, inv_low, sigma_ref):
    values = values_ref[...].reshape(values_ref.shape[0] * 4, 128)
    lane = lanes_of(values.shape)
    high = values.astype(BF16).astype(F32)
    low = values - high
    stacked = []
    for q in range(4):
        left = high if q == 0 else roll(high, 128 - 32 * q)
        right = roll(low, (160 - 32 * q) % 128) if q != 1 else low
        stacked.append(jnp.where(lane < 32, left, right).astype(BF16))
    stacked = jnp.concatenate(stacked, axis=0)
    halves = dot(fwd_high[...], stacked) + dot(fwd_low[...], stacked)
    wave = halves + roll(halves, 96)
    spectrum = spectrum_ref[...]
    cos_a, sin_a, cos_w, sin_w = spectrum[:HALF], spectrum[HALF:], wave[:HALF], wave[HALF:]
    crossed = jnp.concatenate([cos_a * cos_w - sin_a * sin_w, cos_a * sin_w + sin_a * cos_w], axis=0)
    high = crossed.astype(BF16).astype(F32)
    packed = jnp.where(lanes_of(crossed.shape) < 32, high, roll(crossed - high, 32)).astype(BF16)
    halves = dot(inv_high[...], packed) + dot(inv_low[...], packed)
    full = halves + roll(halves, 96)
    sigma_ref[...] = jnp.transpose(full)[:32]


def on_device(peers, sections, g_less, g_greater, partner, pair_rows, pair_weight, source, slab_inverse, coupling):
    own, _, columns = g_less.shape
    energies = own * peers
    orbitals = slab_inverse.shape[-1]
    polar_times = energy_order(peers, own, 4) - energies // 2
    sigma_times = np.arange(energies) + energies // 2
    vmem = pl.BlockSpec(memory_space=pltpu.VMEM)
    hbm = pl.BlockSpec(memory_space=pltpu.HBM)
    square = (orbitals, orbitals)
    strip = (own, orbitals)
    values, spectrum = pl.pallas_call(
        functools.partial(main_kernel, peers, sections),
        out_shape=(
            jax.ShapeDtypeStruct((peers, 4, 128), F32),
            jax.ShapeDtypeStruct((LENGTH, 128), F32),
        ),
        in_specs=[hbm] * 12,
        out_specs=(vmem, vmem),
        scratch_shapes=[
            pltpu.VMEM((128, 128), F32),
            pltpu.VMEM((128, 128), F32),
            pltpu.VMEM((8, 128), jnp.int32),
            pltpu.VMEM((8, 128), jnp.int32),
            pltpu.VMEM((8, 128), F32),
            pltpu.VMEM((1, orbitals), F32),
            pltpu.VMEM(square, F32),
            pltpu.VMEM(square, F32),
            pltpu.VMEM((LENGTH, energies), BF16),
            pltpu.VMEM((LENGTH, energies), BF16),
            pltpu.VMEM((energies, LENGTH), BF16),
            pltpu.VMEM((energies, LENGTH), BF16),
            pltpu.SemaphoreType.DMA((12,)),
            pltpu.VMEM((128, 128), F32),
            pltpu.VMEM((peers, 8, 128), F32),
            pltpu.VMEM((peers, 8, 128), F32),
            pltpu.VMEM((peers, 4, 128), F32),
            pltpu.VMEM((peers, 4, 128), F32),
            pltpu.VMEM((peers, 4, 128), F32),
            pltpu.VMEM((orbitals, columns), BF16),
            pltpu.VMEM(square, BF16),
            pltpu.VMEM(square, BF16),
            pltpu.VMEM(square, BF16),
            pltpu.VMEM(square, BF16),
            pltpu.VMEM((REACH, 2, orbitals // 2, orbitals), F32),
            pltpu.VMEM((REACH - 1, orbitals // 2, orbitals), F32),
            pltpu.VMEM((REACH,) + square, BF16),
            pltpu.VMEM((REACH,) + square, BF16),
            pltpu.SemaphoreType.DMA((REACH, 2)),
            pltpu.SemaphoreType.DMA((REACH, 2)),
            pltpu.SemaphoreType.DMA((REACH, 2)),
            pltpu.SemaphoreType.DMA((REACH, 2)),
            pltpu.VMEM(strip, F32),
            pltpu.VMEM(strip, F32),
            pltpu.VMEM(strip, F32),
            pltpu.VMEM((REACH + 1,) + strip, F32),
            pltpu.SemaphoreType.DMA((REACH + 1,)),
            pltpu.SemaphoreType.DMA((REACH + 1,)),
        ]
        + [pltpu.SemaphoreType.DMA] * 6,
        compiler_params=pltpu.CompilerParams(
            collective_id=0, has_side_effects=True, vmem_limit_bytes=60 * 1024 * 1024
        ),
        name="update",
    )(
        g_less.reshape(-1, 128),
        g_greater.reshape(-1, 128),
        partner.reshape(-1, 128),
        pair_rows.reshape(-1, 128),
        pair_weight.reshape(-1, 128),
        source,
        slab_inverse[0],
        coupling[0],
        *forward_table(energy_order(peers, own, 2)),
        *inverse_table(polar_times, energies),
    )
    sigma = pl.pallas_call(
        last_kernel,
        out_shape=jax.ShapeDtypeStruct((columns // peers, energies), F32),
        in_specs=[vmem] * 6,
        out_specs=vmem,
        compiler_params=pltpu.CompilerParams(vmem_limit_bytes=32 * 1024 * 1024),
        name="convolution",
    )(
        values,
        spectrum,
        *forward_table(energy_order(peers, own, 4)),
        *inverse_table(sigma_times, energies),
    )
    return jnp.transpose(sigma)[:, None, :]


def solution(mesh):
    return jax.shard_map(
        functools.partial(on_device, mesh.shape["energy"], mesh.shape["section"]),
        mesh=mesh,
        in_specs=(
            P("energy", "section", None),
            P("energy", "section", None),
            P("section", None),
            P("section", None),
            P("section", None),
            P("section", None),
            P("section", None, None),
            P("section", None, None),
        ),
        out_specs=P(None, "section", "energy"),
        check_vma=False,
    )
```

```python
import functools
import math

import jax
import jax.numpy as jnp
import numpy as np
from jax import lax
from jax.experimental import pallas as pl
from jax.experimental.pallas import tpu as pltpu
from jax.sharding import PartitionSpec as P

MESH = pl.DeviceIdType.MESH
F32 = jnp.float32
BF16 = jnp.bfloat16
NT = (((1,), (1,)), ((), ()))
NN = (((1,), (0,)), ((), ()))
LENGTH = 768
HALF = LENGTH // 2
REACH = 4


def two_parts(table):
    table = np.asarray(table, np.float32)
    high = table.astype(jnp.bfloat16)
    low = (table - high.astype(np.float32)).astype(jnp.bfloat16)
    return jnp.asarray(high), jnp.asarray(low)


def angles(times):
    return np.outer(np.arange(HALF) + 0.5, np.asarray(times, np.float64)) * (2.0 * math.pi / LENGTH)


def forward_table(order):
    phase = angles(order)
    return two_parts(np.concatenate([np.cos(phase), np.sin(phase)], axis=0))


def inverse_table(times, energies):
    phase = angles(times).T
    scale = 2.0 / LENGTH / math.sqrt(energies)
    return two_parts(np.concatenate([np.cos(phase), np.sin(phase)], axis=1) * scale)


def energy_order(peers, own, fold):
    rows = own // fold
    group, sender, row = np.meshgrid(np.arange(fold), np.arange(peers), np.arange(rows), indexing="ij")
    return (sender * own + group * rows + row).reshape(-1)


def lanes_of(shape):
    return lax.broadcasted_iota(jnp.int32, shape, len(shape) - 1)


def roll(x, shift, axis=1):
    return pltpu.roll(x, shift, axis)


def exchange_groups(parts):
    a0, a1, a2, a3 = parts
    lane = lanes_of(a0.shape)
    low = lane < 64
    near = lane % 64 < 32
    b0, b2 = jnp.where(low, a0, roll(a2, 64)), jnp.where(low, roll(a0, 64), a2)
    b1, b3 = jnp.where(low, a1, roll(a3, 64)), jnp.where(low, roll(a1, 64), a3)
    c0, c1 = jnp.where(near, b0, roll(b1, 32)), jnp.where(near, roll(b0, 96), b1)
    c2, c3 = jnp.where(near, b2, roll(b3, 32)), jnp.where(near, roll(b2, 96), b3)
    return c0, c1, c2, c3


def exchange_rows(first, second):
    lane = lanes_of(first.shape)
    row = lax.broadcasted_iota(jnp.int32, first.shape, 0)
    low = lane < 64
    upper_half = row < 4
    keep = (lane % 64 < 32) == upper_half
    one, two = jnp.where(low, first, roll(second, 64)), jnp.where(low, roll(first, 64), second)

    def inside(x):
        turned = roll(x, 4, 0)
        return jnp.where(keep, x, jnp.where(upper_half, roll(turned, 32), roll(turned, 96)))

    return inside(one), inside(two)


def split(x):
    high = x.astype(BF16)
    return high, (x - high.astype(F32)).astype(BF16)


def dot(x, y, dims=NN):
    return lax.dot_general(x, y, dims, preferred_element_type=F32)


def product(x, high, low, dims):
    rows = x.shape[0]
    x_high, x_low = split(x)
    both = dot(jnp.concatenate([x_high, x_low], axis=0), high, dims)
    return both[:rows] + both[rows:] + dot(x_high, low, dims)


def far_first(peers, n):
    return peers // 2 + (n + 1) // 2 * (1 - n % 2 * 2)


def scatter_start(peers, me, source, target, send, recv):
    def one(n, _):
        peer = lax.rem(me + far_first(peers, n), peers)
        pltpu.make_async_remote_copy(
            src_ref=source.at[peer],
            dst_ref=target.at[me],
            send_sem=send,
            recv_sem=recv,
            device_id={"energy": peer},
            device_id_type=MESH,
        ).start()
        return 0

    lax.fori_loop(0, peers - 1, one, 0)
    target[me] = source[me]


def wait_blocks(peers, ref, semaphore):
    part = ref.at[pl.ds(0, peers - 1)]
    pltpu.make_async_copy(part, part, semaphore).wait()


def chunk_rows(chunk):
    return slice(0, 128) if chunk == 0 else slice(128, 208)


def fold_rest(rows):
    count, columns = rows.shape
    tail = rows[:, columns // 128 * 128 :]
    tail = jnp.concatenate([tail, jnp.zeros((count, 128 - tail.shape[1]), F32)], axis=1)
    if count < 128:
        tail = jnp.concatenate([tail, jnp.zeros((128 - count, 128), F32)], axis=0)
    group = lanes_of((32, 128)) // 32
    folded = tail[:32]
    for g in range(1, 4):
        folded = jnp.where(group == g, roll(tail[32 * g : 32 * g + 32], 32 * g), folded)
    return folded


def unfold_rest(folded, count):
    groups = [folded] + [roll(folded, 128 - 32 * g) for g in range(1, 4)]
    return jnp.concatenate(groups, axis=0)[:count, :32]


def lane_take(x, index):
    return jnp.take_along_axis(x, index, axis=1, mode="promise_in_bounds")


def main_kernel(
    peers, sections,
    less_hbm, great_hbm, partner_hbm, rows_hbm, weight_hbm, source_hbm, inverse_hbm, coupling_hbm,
    fwd_high_hbm, fwd_low_hbm, inv_high_hbm, inv_low_hbm,
    values_out, spectrum_out,
    less_ref, great_ref, partner_ref, rows_ref, weight_ref, source_ref, inverse_ref, coupling_ref,
    fwd_high, fwd_low, inv_high, inv_low, load_sem,
    swapped, first_send, first_recv, second_send, second_recv, third_send,
    orbital_table, slab_high, slab_low, couple_high, couple_low,
    steps, inbox, rest, rest_in, step_high, step_low, next_send, next_recv, twin_send, twin_recv,
    upward, offset, carried, arrived, across_send, across_recv,
    send_one, recv_one, send_two, recv_two, send_three, recv_three,
):
    me = lax.axis_index("energy")
    section = lax.axis_index("section")
    has_before = section > 0
    has_after = section < sections - 1
    after = lax.rem(section + 1, sections)
    orbitals = inverse_ref.shape[0]
    half, full = orbitals // 2, orbitals // 128 * 128
    core = lax.rem(me, 2)
    twin = me + 1 - 2 * core

    loads = [
        pltpu.make_async_copy(source, target, load_sem.at[place])
        for place, (source, target) in enumerate((
            (great_hbm, great_ref), (partner_hbm, partner_ref), (less_hbm, less_ref), (rows_hbm, rows_ref),
            (weight_hbm, weight_ref), (source_hbm, source_ref), (inverse_hbm, inverse_ref),
            (coupling_hbm, coupling_ref), (fwd_high_hbm, fwd_high), (fwd_low_hbm, fwd_low),
            (inv_high_hbm, inv_high), (inv_low_hbm, inv_low),
        ))
    ]
    for load in loads:
        load.start()

    barrier = pltpu.get_barrier_semaphore()

    def greet(n, _):
        peer = lax.rem(me + far_first(peers, n), peers)
        pl.semaphore_signal(barrier, inc=1, device_id={"energy": peer}, device_id_type=MESH)
        return 0

    lax.fori_loop(0, peers - 1, greet, 0)

    for away in range(1, REACH + 1):
        for there, other in ((section >= away, section - away), (section < sections - away, section + away)):

            @pl.when(there)
            def _(other=other):
                pl.semaphore_signal(barrier, inc=1, device_id={"section": other}, device_id_type=MESH)

    loads[0].wait()
    loads[1].wait()
    loads[2].wait()

    partner = partner_ref[...]
    partner_tile, partner_lane = partner // 128, partner % 128
    for energy in range(16):
        total = jnp.zeros((8, 128), F32)
        for tile in range(8):
            line = jnp.broadcast_to(great_ref[8 * energy + tile : 8 * energy + tile + 1, :], (8, 128))
            total = jnp.where(partner_tile == tile, lane_take(line, partner_lane), total)
        swapped[8 * energy : 8 * energy + 8, :] = total

    for tile in range(8):
        parts = []
        for h in range(2):
            for ref in (less_ref, swapped):
                parts.append(ref[pl.ds(64 * h + tile, 8, stride=8), :])
        for b, part in enumerate(exchange_groups(parts)):
            first_send[4 * tile + b] = part

    for load in loads[3:8]:
        load.wait()
    slab_high[...], slab_low[...] = split(inverse_ref[...])
    couple_high[...], couple_low[...] = split(coupling_ref[...])
    slab_map = (
        dot(slab_high[...], couple_high[...])
        + dot(slab_high[...], couple_low[...])
        + dot(slab_low[...], couple_high[...])
    )
    map_high, map_low = split(slab_map)
    index = lax.broadcasted_iota(jnp.int32, (orbitals, orbitals), 0)
    identity = (index == lanes_of((orbitals, orbitals))).astype(F32).astype(BF16)
    turned_high, turned_low = dot(identity, map_high, NT), dot(identity, map_low, NT)
    step_high[0], step_low[0] = turned_high.astype(BF16), turned_low.astype(BF16)
    turned = turned_high + turned_low
    steps[0, 0], steps[0, 1] = turned[:half], turned[half:]
    own_half = steps[0, core]
    for chunk in range(2):
        rest[0, chunk] = fold_rest(own_half[chunk_rows(chunk)])

    pl.semaphore_wait(barrier, peers - 1 + jnp.minimum(section, REACH) + jnp.minimum(sections - 1 - section, REACH))
    scatter_start(peers, me, first_send, first_recv, send_one, recv_one)

    def rows_of(chunk):
        rows = chunk_rows(chunk)
        return pl.ds(rows.start, rows.stop - rows.start)

    def to_next(k, chunk):
        def copy(source, target, place):
            return pltpu.make_async_remote_copy(
                src_ref=source,
                dst_ref=target,
                send_sem=next_send.at[k - 1, chunk, place],
                recv_sem=next_recv.at[k - 1, chunk, place],
                device_id={"section": after},
                device_id_type=MESH,
            )

        whole = pl.ds(0, full)
        return (
            copy(steps.at[k - 1, core, rows_of(chunk), whole], inbox.at[k - 1, rows_of(chunk)], 0),
            copy(rest.at[k - 1, chunk], rest_in.at[k - 1, chunk], 1),
        )

    def to_twin(k, chunk):
        return pltpu.make_async_remote_copy(
            src_ref=steps.at[k - 1, core, rows_of(chunk)],
            dst_ref=steps.at[k - 1, core, rows_of(chunk)],
            send_sem=twin_send.at[k - 1, chunk],
            recv_sem=twin_recv.at[k - 1, chunk],
            device_id={"energy": twin},
            device_id_type=MESH,
        )

    def pass_on(k, chunk):
        @pl.when(has_after)
        def _():
            for copy in to_next(k, chunk):
                copy.start()

    def grow(k, chunk):
        @pl.when(has_before)
        def _():
            for copy in to_next(k - 1, chunk):
                copy.wait_recv()

        rows = rows_of(chunk)
        last = unfold_rest(rest_in[k - 2, chunk], rows.size)
        high, low = split(jnp.concatenate([inbox[k - 2, rows], last], axis=1))
        whole_high, whole_low = step_high[0], step_low[0]
        grown = dot(high, whole_high) + dot(low, whole_high) + dot(high, whole_low)
        steps[k - 1, core, rows] = grown
        if k < REACH:
            rest[k - 1, chunk] = fold_rest(grown)
            pass_on(k, chunk)
        to_twin(k, chunk).start()

    def gather(k):
        for chunk in range(2):
            to_twin(k, chunk).wait_recv()
        for part in range(2):
            rows = pl.ds(half * part, half)
            step_high[k - 1, rows], step_low[k - 1, rows] = split(steps[k - 1, part])

    @pl.when(jnp.logical_not(has_before))
    def _():
        inbox[...] = jnp.zeros_like(inbox)
        rest_in[...] = jnp.zeros_like(rest_in)

    for chunk in range(2):
        pass_on(1, chunk)

    pair_rows = rows_ref[...]
    for tile in range(8):
        index = lax.broadcasted_iota(jnp.int32, (orbitals, 128), 0)
        orbital_table[:, 128 * tile : 128 * tile + 128] = (
            (index == pair_rows[tile : tile + 1, :]).astype(F32).astype(BF16)
        )
    source = source_ref[...]
    base = product(jnp.broadcast_to(source, (16, orbitals)), slab_high[...], slab_low[...], NT)
    grow(2, 0)

    for load in loads[8:]:
        load.wait()
    wait_blocks(peers, first_recv, recv_one)

    blocks = first_recv[...].reshape(peers * 8, 128)
    low_lanes = lanes_of(blocks.shape) < 64
    high = blocks.astype(BF16).astype(F32)
    low = blocks - high
    stacked = jnp.concatenate(
        [
            jnp.where(low_lanes, high, roll(low, 64)).astype(BF16),
            jnp.where(low_lanes, roll(high, 64), low).astype(BF16),
        ],
        axis=0,
    )
    halves = dot(fwd_high[...], stacked) + dot(fwd_low[...], stacked)
    spectrum = halves + roll(halves, 64)
    spectrum_out[...] = spectrum
    other = roll(spectrum, 96)
    cos_a, sin_a, cos_b, sin_b = spectrum[:HALF], spectrum[HALF:], other[:HALF], other[HALF:]
    crossed = jnp.concatenate([cos_a * cos_b + sin_a * sin_b, sin_a * cos_b - cos_a * sin_b], axis=0)
    high = crossed.astype(BF16).astype(F32)
    packed = jnp.where(lanes_of(crossed.shape) < 32, high, roll(crossed - high, 32)).astype(BF16)
    halves = dot(inv_high[...], packed) + dot(inv_low[...], packed)
    polar = halves + roll(halves, 96)
    count = polar.shape[0] // 4
    group = lanes_of((count, 128)) // 32
    joined = polar[:count]
    for q in range(1, 4):
        joined = jnp.where(group == q, roll(polar[count * q : count * (q + 1)], 32 * q), joined)
    second_send[...] = joined.reshape(peers, 4, 128)
    scatter_start(peers, me, second_send, second_recv, send_two, recv_two)
    grow(2, 1)
    grow(3, 0)
    gather(2)
    grow(3, 1)
    gather(3)
    wait_blocks(peers, second_recv, recv_two)

    weighted = []
    for tile in range(8):
        lines = [second_recv[4 * tile + b] for b in range(4)]
        one, two = exchange_rows(jnp.concatenate(lines[:2], axis=0), jnp.concatenate(lines[2:], axis=0))
        weighted.append(jnp.concatenate([one, two], axis=0) * weight_ref[tile : tile + 1, :])
    both = dot(jnp.concatenate(split(jnp.concatenate(weighted, axis=1)), axis=0), orbital_table[...], NT)
    local_pol = both[:16] + both[16:]
    guess = base + product(local_pol * base, slab_high[...], slab_low[...], NT)
    upward[...] = product(guess, couple_high[...], couple_low[...], NN)

    def across(source, place, away):
        return pltpu.make_async_remote_copy(
            src_ref=source,
            dst_ref=arrived.at[place],
            send_sem=across_send.at[place],
            recv_sem=across_recv.at[place],
            device_id={"section": lax.rem(section + sections + away, sections)},
            device_id_type=MESH,
        )

    shift = across(upward, 0, -1)
    window = [across(offset, away, away) for away in range(1, REACH)]
    sweep = across(carried, REACH, REACH)

    @pl.when(has_before)
    def _():
        shift.start()

    grow(4, 0)
    partial = source + local_pol * guess

    @pl.when(has_after)
    def _():
        shift.wait_recv()

    @pl.when(jnp.logical_not(has_after))
    def _():
        arrived[0] = jnp.zeros_like(upward)

    offset[...] = product(partial + arrived[0], slab_high[...], slab_low[...], NT)
    for away in range(1, REACH):

        @pl.when(section < sections - away)
        def _(away=away):
            window[away - 1].start()

    grow(4, 1)
    gather(4)
    carried[...] = offset[...]
    for away in range(1, REACH):

        @pl.when(section >= away)
        def _(away=away):
            window[away - 1].wait_recv()
            carried[...] += product(arrived[away], step_high[away - 1], step_low[away - 1], NN)

    @pl.when(section < REACH)
    def _():
        sweep.start()


    @pl.when(section >= REACH)
    def _():
        sweep.wait_recv()
        carried[...] += product(arrived[REACH], step_high[REACH - 1], step_low[REACH - 1], NN)

        @pl.when(section < sections - REACH)
        def _():
            sweep.start()

    screened = carried[...]
    both = dot(jnp.concatenate(split(screened), axis=0), orbital_table[...])
    pairs = both[:16] + both[16:]
    for tile in range(8):
        piece = pairs[:, 128 * tile : 128 * tile + 128] * weight_ref[tile : tile + 1, :]
        one, two = exchange_rows(piece[:8], piece[8:])
        for b, block in enumerate((one[:4], one[4:], two[:4], two[4:])):
            third_send[4 * tile + b] = block
    scatter_start(peers, me, third_send, values_out, send_three, recv_three)

    @pl.when(has_before)
    def _():
        shift.wait_send()

    for away in range(1, REACH):

        @pl.when(section < sections - away)
        def _(away=away):
            window[away - 1].wait_send()

    @pl.when(section < sections - REACH)
    def _():
        sweep.wait_send()

    for chunk in range(2):

        @pl.when(has_after)
        def _(chunk=chunk):
            for k in range(1, REACH):
                for copy in to_next(k, chunk):
                    copy.wait_send()

        for k in range(2, REACH + 1):
            to_twin(k, chunk).wait_send()

    wait_blocks(peers, first_send, send_one)
    wait_blocks(peers, second_send, send_two)
    wait_blocks(peers, third_send, send_three)
    wait_blocks(peers, values_out, recv_three)


def last_kernel(values_ref, spectrum_ref, fwd_high, fwd_low, inv_high, inv_low, sigma_ref):
    values = values_ref[...].reshape(values_ref.shape[0] * 4, 128)
    lane = lanes_of(values.shape)
    high = values.astype(BF16).astype(F32)
    low = values - high
    stacked = []
    for q in range(4):
        left = high if q == 0 else roll(high, 128 - 32 * q)
        right = roll(low, (160 - 32 * q) % 128) if q != 1 else low
        stacked.append(jnp.where(lane < 32, left, right).astype(BF16))
    stacked = jnp.concatenate(stacked, axis=0)
    halves = dot(fwd_high[...], stacked) + dot(fwd_low[...], stacked)
    wave = halves + roll(halves, 96)
    spectrum = spectrum_ref[...]
    cos_a, sin_a, cos_w, sin_w = spectrum[:HALF], spectrum[HALF:], wave[:HALF], wave[HALF:]
    crossed = jnp.concatenate([cos_a * cos_w - sin_a * sin_w, cos_a * sin_w + sin_a * cos_w], axis=0)
    high = crossed.astype(BF16).astype(F32)
    packed = jnp.where(lanes_of(crossed.shape) < 32, high, roll(crossed - high, 32)).astype(BF16)
    halves = dot(inv_high[...], packed) + dot(inv_low[...], packed)
    full = halves + roll(halves, 96)
    sigma_ref[...] = jnp.transpose(full)[:32]


def on_device(peers, sections, g_less, g_greater, partner, pair_rows, pair_weight, source, slab_inverse, coupling):
    own, _, columns = g_less.shape
    energies = own * peers
    orbitals = slab_inverse.shape[-1]
    polar_times = energy_order(peers, own, 4) - energies // 2
    sigma_times = np.arange(energies) + energies // 2
    vmem = pl.BlockSpec(memory_space=pltpu.VMEM)
    hbm = pl.BlockSpec(memory_space=pltpu.HBM)
    square = (orbitals, orbitals)
    strip = (own, orbitals)
    values, spectrum = pl.pallas_call(
        functools.partial(main_kernel, peers, sections),
        out_shape=(
            jax.ShapeDtypeStruct((peers, 4, 128), F32),
            jax.ShapeDtypeStruct((LENGTH, 128), F32),
        ),
        in_specs=[hbm] * 12,
        out_specs=(vmem, vmem),
        scratch_shapes=[
            pltpu.VMEM((128, 128), F32),
            pltpu.VMEM((128, 128), F32),
            pltpu.VMEM((8, 128), jnp.int32),
            pltpu.VMEM((8, 128), jnp.int32),
            pltpu.VMEM((8, 128), F32),
            pltpu.VMEM((1, orbitals), F32),
            pltpu.VMEM(square, F32),
            pltpu.VMEM(square, F32),
            pltpu.VMEM((LENGTH, energies), BF16),
            pltpu.VMEM((LENGTH, energies), BF16),
            pltpu.VMEM((energies, LENGTH), BF16),
            pltpu.VMEM((energies, LENGTH), BF16),
            pltpu.SemaphoreType.DMA((12,)),
            pltpu.VMEM((128, 128), F32),
            pltpu.VMEM((peers, 8, 128), F32),
            pltpu.VMEM((peers, 8, 128), F32),
            pltpu.VMEM((peers, 4, 128), F32),
            pltpu.VMEM((peers, 4, 128), F32),
            pltpu.VMEM((peers, 4, 128), F32),
            pltpu.VMEM((orbitals, columns), BF16),
            pltpu.VMEM(square, BF16),
            pltpu.VMEM(square, BF16),
            pltpu.VMEM(square, BF16),
            pltpu.VMEM(square, BF16),
            pltpu.VMEM((REACH, 2, orbitals // 2, orbitals), F32),
            pltpu.VMEM((REACH - 1, orbitals // 2, orbitals // 128 * 128), F32),
            pltpu.VMEM((REACH - 1, 2, 32, 128), F32),
            pltpu.VMEM((REACH - 1, 2, 32, 128), F32),
            pltpu.VMEM((REACH,) + square, BF16),
            pltpu.VMEM((REACH,) + square, BF16),
            pltpu.SemaphoreType.DMA((REACH, 2, 2)),
            pltpu.SemaphoreType.DMA((REACH, 2, 2)),
            pltpu.SemaphoreType.DMA((REACH, 2)),
            pltpu.SemaphoreType.DMA((REACH, 2)),
            pltpu.VMEM(strip, F32),
            pltpu.VMEM(strip, F32),
            pltpu.VMEM(strip, F32),
            pltpu.VMEM((REACH + 1,) + strip, F32),
            pltpu.SemaphoreType.DMA((REACH + 1,)),
            pltpu.SemaphoreType.DMA((REACH + 1,)),
        ]
        + [pltpu.SemaphoreType.DMA] * 6,
        compiler_params=pltpu.CompilerParams(
            collective_id=0, has_side_effects=True, vmem_limit_bytes=60 * 1024 * 1024
        ),
        name="update",
    )(
        g_less.reshape(-1, 128),
        g_greater.reshape(-1, 128),
        partner.reshape(-1, 128),
        pair_rows.reshape(-1, 128),
        pair_weight.reshape(-1, 128),
        source,
        slab_inverse[0],
        coupling[0],
        *forward_table(energy_order(peers, own, 2)),
        *inverse_table(polar_times, energies),
    )
    sigma = pl.pallas_call(
        last_kernel,
        out_shape=jax.ShapeDtypeStruct((columns // peers, energies), F32),
        in_specs=[vmem] * 6,
        out_specs=vmem,
        compiler_params=pltpu.CompilerParams(vmem_limit_bytes=32 * 1024 * 1024),
        name="convolution",
    )(
        values,
        spectrum,
        *forward_table(energy_order(peers, own, 4)),
        *inverse_table(sigma_times, energies),
    )
    return jnp.transpose(sigma)[:, None, :]


def solution(mesh):
    return jax.shard_map(
        functools.partial(on_device, mesh.shape["energy"], mesh.shape["section"]),
        mesh=mesh,
        in_specs=(
            P("energy", "section", None),
            P("energy", "section", None),
            P("section", None),
            P("section", None),
            P("section", None),
            P("section", None),
            P("section", None, None),
            P("section", None, None),
        ),
        out_specs=P(None, "section", "energy"),
        check_vma=False,
    )
```

```python
import functools
import math

import jax
import jax.numpy as jnp
import numpy as np
from jax import lax
from jax.experimental import pallas as pl
from jax.experimental.pallas import tpu as pltpu
from jax.sharding import PartitionSpec as P

MESH = pl.DeviceIdType.MESH
F32 = jnp.float32
BF16 = jnp.bfloat16
NT = (((1,), (1,)), ((), ()))
NN = (((1,), (0,)), ((), ()))
LENGTH = 768
HALF = LENGTH // 2
REACH = 4


def two_parts(table):
    table = np.asarray(table, np.float32)
    high = table.astype(jnp.bfloat16)
    low = (table - high.astype(np.float32)).astype(jnp.bfloat16)
    return jnp.asarray(high), jnp.asarray(low)


def angles(order, energies):
    times = np.asarray(order, np.float64) - (energies - 1) / 2
    return np.outer(np.arange(HALF) + 0.5, times) * (2.0 * math.pi / LENGTH)


def forward_table(order, energies):
    phase = angles(order, energies)
    return two_parts(np.concatenate([np.cos(phase), np.sin(phase)], axis=0))


def inverse_table(order, energies):
    phase = angles(order, energies).T
    scale = 2.0 / LENGTH / math.sqrt(energies)
    return two_parts(np.concatenate([np.cos(phase), np.sin(phase)], axis=0) * scale)


def half_steps():
    phase = (np.arange(HALF) + 0.5) * (math.pi / LENGTH)
    table = np.concatenate([np.cos(phase), np.sin(phase)])
    return jnp.asarray(np.broadcast_to(table[:, None], (LENGTH, 128)).astype(np.float32))


def energy_order(peers, own, fold):
    rows = own // fold
    group, sender, row = np.meshgrid(np.arange(fold), np.arange(peers // 2), np.arange(rows), indexing="ij")
    return (sender * own + group * rows + row).reshape(-1)


def lanes_of(shape):
    return lax.broadcasted_iota(jnp.int32, shape, len(shape) - 1)


def roll(x, shift, axis=1):
    return pltpu.roll(x, shift, axis)


def exchange_groups(parts):
    a0, a1, a2, a3 = parts
    lane = lanes_of(a0.shape)
    low = lane < 64
    near = lane % 64 < 32
    b0, b2 = jnp.where(low, a0, roll(a2, 64)), jnp.where(low, roll(a0, 64), a2)
    b1, b3 = jnp.where(low, a1, roll(a3, 64)), jnp.where(low, roll(a1, 64), a3)
    c0, c1 = jnp.where(near, b0, roll(b1, 32)), jnp.where(near, roll(b0, 96), b1)
    c2, c3 = jnp.where(near, b2, roll(b3, 32)), jnp.where(near, roll(b2, 96), b3)
    return c0, c1, c2, c3


def exchange_rows(first, second):
    lane = lanes_of(first.shape)
    row = lax.broadcasted_iota(jnp.int32, first.shape, 0)
    low = lane < 64
    upper_half = row < 4
    keep = (lane % 64 < 32) == upper_half
    one, two = jnp.where(low, first, roll(second, 64)), jnp.where(low, roll(first, 64), second)

    def inside(x):
        turned = roll(x, 4, 0)
        return jnp.where(keep, x, jnp.where(upper_half, roll(turned, 32), roll(turned, 96)))

    return inside(one), inside(two)


def split(x):
    high = x.astype(BF16)
    return high, (x - high.astype(F32)).astype(BF16)


def dot(x, y, dims=NN):
    return lax.dot_general(x, y, dims, preferred_element_type=F32)


def product(x, high, low, dims):
    rows = x.shape[0]
    x_high, x_low = split(x)
    both = dot(jnp.concatenate([x_high, x_low], axis=0), high, dims)
    return both[:rows] + both[rows:] + dot(x_high, low, dims)


def far_first(peers, n):
    return peers // 2 + (n + 1) // 2 * (1 - n % 2 * 2)


def scatter_start(peers, me, source, target, send, recv, source_place, target_place):
    mine = target_place(me)

    def one(n, _):
        peer = lax.rem(me + far_first(peers, n), peers)
        pltpu.make_async_remote_copy(
            src_ref=source.at[source_place(peer)],
            dst_ref=target.at[mine],
            send_sem=send,
            recv_sem=recv,
            device_id={"energy": peer},
            device_id_type=MESH,
        ).start()
        return 0

    lax.fori_loop(0, peers - 1, one, 0)
    target[mine] = source[source_place(me)]


def wait_blocks(peers, ref, semaphore):
    part = ref.at[pl.ds(0, peers - 1)]
    pltpu.make_async_copy(part, part, semaphore).wait()


def chunk_rows(chunk):
    return slice(0, 128) if chunk == 0 else slice(128, 208)


def fold_rest(rows):
    count, columns = rows.shape
    tail = rows[:, columns // 128 * 128 :]
    tail = jnp.concatenate([tail, jnp.zeros((count, 128 - tail.shape[1]), F32)], axis=1)
    if count < 128:
        tail = jnp.concatenate([tail, jnp.zeros((128 - count, 128), F32)], axis=0)
    group = lanes_of((32, 128)) // 32
    folded = tail[:32]
    for g in range(1, 4):
        folded = jnp.where(group == g, roll(tail[32 * g : 32 * g + 32], 32 * g), folded)
    return folded


def unfold_rest(folded, count):
    groups = [folded] + [roll(folded, 128 - 32 * g) for g in range(1, 4)]
    return jnp.concatenate(groups, axis=0)[:count, :32]


def backward(inv_high, inv_low, real, turned):
    def one(rows, x):
        high = x.astype(BF16).astype(F32)
        packed = jnp.where(lanes_of(x.shape) < 32, high, roll(x - high, 32)).astype(BF16)
        halves = dot(inv_high[rows], packed) + dot(inv_low[rows], packed)
        return halves + roll(halves, 96)

    count = inv_high.shape[0] // 2
    return one(pl.ds(0, count), real), one(pl.ds(count, count), turned)


def lane_take(x, index):
    return jnp.take_along_axis(x, index, axis=1, mode="promise_in_bounds")


def convolve(values_ref, spectrum_ref, fwd_high, fwd_low, inv_high, inv_low, half_step, sigma_ref):
    senders = values_ref.shape[0] // 2
    first = values_ref[:senders].reshape(senders * 4, 128)
    second = values_ref[senders:].reshape(senders * 4, 128)
    lane = lanes_of(first.shape)

    def parts_of(x):
        high = x.astype(BF16).astype(F32)
        low = x - high
        stacked = []
        for q in range(4):
            left = high if q == 0 else roll(high, 128 - 32 * q)
            right = low if q == 1 else roll(low, (160 - 32 * q) % 128)
            stacked.append(jnp.where(lane < 32, left, right))
        return jnp.concatenate(stacked, axis=0).astype(BF16)

    def forward(rows, x):
        halves = dot(fwd_high[rows], x) + dot(fwd_low[rows], x)
        return halves + roll(halves, 96)

    cosines, sines = pl.ds(0, HALF), pl.ds(HALF, HALF)
    cos_w, sin_w = forward(cosines, parts_of(first + second)), forward(sines, parts_of(first - second))
    cos_a, sin_a = spectrum_ref[cosines], spectrum_ref[sines]
    real, turned = cos_a * cos_w - sin_a * sin_w, cos_a * sin_w + sin_a * cos_w
    cos_half, sin_half = half_step[cosines], half_step[sines]
    even, odd = backward(
        inv_high, inv_low, real * cos_half + turned * sin_half, turned * cos_half - real * sin_half
    )
    count = even.shape[0]
    later = even - odd
    lane = lanes_of(later.shape)
    high = later.astype(BF16).astype(F32)
    middle = (later - high).astype(BF16).astype(F32)
    low = later - high - middle
    packed = jnp.where(lane < 32, high, jnp.where(lane < 64, roll(middle, 32), roll(low, 64))).astype(BF16)
    row = lax.broadcasted_iota(jnp.int32, (count, count), 0)
    reverse = (row + lanes_of((count, count)) == count - 1).astype(F32).astype(BF16)
    turned_round = dot(reverse, packed)
    later = turned_round + roll(turned_round, 96) + roll(turned_round, 64)
    sigma_ref[:, :count] = jnp.transpose(even + odd)[:32]
    sigma_ref[:, count:] = jnp.transpose(later)[:32]


def main_kernel(
    peers, sections,
    less_hbm, great_hbm, partner_hbm, rows_hbm, weight_hbm, source_hbm, inverse_hbm, coupling_hbm,
    fwd_high_hbm, fwd_low_hbm, inv_high_hbm, inv_low_hbm, step_hbm,
    last_fwd_high_hbm, last_fwd_low_hbm, last_inv_high_hbm, last_inv_low_hbm,
    sigma_out,
    less_ref, great_ref, partner_ref, rows_ref, weight_ref, source_ref, inverse_ref, coupling_ref,
    fwd_high, fwd_low, inv_high, inv_low, half_step,
    last_fwd_high, last_fwd_low, last_inv_high, last_inv_low, load_sem,
    values, spectrum,
    swapped, ordered, first_send, first_recv, second_send, second_recv, third_send,
    orbital_table, slab_high, slab_low, couple_high, couple_low, lift_high, lift_low,
    steps, inbox, rest, rest_in, step_high, step_low, next_send, next_recv, twin_send, twin_recv,
    upward, offset, carried, arrived, across_send, across_recv,
    send_one, recv_one, send_two, recv_two, send_three, recv_three,
):
    me = lax.axis_index("energy")
    section = lax.axis_index("section")
    has_before = section > 0
    has_after = section < sections - 1
    after = lax.rem(section + 1, sections)
    orbitals = inverse_ref.shape[0]
    half, full = orbitals // 2, orbitals // 128 * 128
    core = lax.rem(me, 2)
    in_upper = me >= peers // 2

    def as_is(place):
        return place

    def mirrored(place):
        return jnp.where(place < peers // 2, place, 3 * peers // 2 - 1 - place)

    twin = me + 1 - 2 * core

    barrier = pltpu.get_barrier_semaphore()

    def greet(n, _):
        peer = lax.rem(me + far_first(peers, n), peers)
        pl.semaphore_signal(barrier, inc=1, device_id={"energy": peer}, device_id_type=MESH)
        return 0

    lax.fori_loop(0, peers - 1, greet, 0)

    for away in range(1, REACH + 1):
        for there, other in ((section >= away, section - away), (section < sections - away, section + away)):

            @pl.when(there)
            def _(other=other):
                pl.semaphore_signal(barrier, inc=1, device_id={"section": other}, device_id_type=MESH)

    loads = [
        pltpu.make_async_copy(source, target, load_sem.at[place])
        for place, (source, target) in enumerate((
            (great_hbm, great_ref), (partner_hbm, partner_ref), (less_hbm, less_ref), (rows_hbm, rows_ref),
            (weight_hbm, weight_ref), (source_hbm, source_ref), (inverse_hbm, inverse_ref),
            (coupling_hbm, coupling_ref), (fwd_high_hbm, fwd_high), (fwd_low_hbm, fwd_low),
            (inv_high_hbm, inv_high), (inv_low_hbm, inv_low),
            (step_hbm, half_step),
            (last_fwd_high_hbm, last_fwd_high), (last_fwd_low_hbm, last_fwd_low),
            (last_inv_high_hbm, last_inv_high), (last_inv_low_hbm, last_inv_low),
        ))
    ]
    for load in loads:
        load.start()

    for load in loads[:3]:
        load.wait()

    partner = partner_ref[...]
    partner_tile, partner_lane = partner // 128, partner % 128
    for place in range(16):
        energy = pl.ds(pl.multiple_of(8 * jnp.where(in_upper, 15 - place, place), 8), 8)
        lines = great_ref[energy, :]
        total = jnp.zeros((8, 128), F32)
        for tile in range(8):
            line = jnp.broadcast_to(lines[tile : tile + 1, :], (8, 128))
            total = jnp.where(partner_tile == tile, lane_take(line, partner_lane), total)
        swapped[8 * place : 8 * place + 8, :] = total
        ordered[8 * place : 8 * place + 8, :] = less_ref[energy, :]

    for tile in range(8):
        parts = []
        for h in range(2):
            for ref in (ordered, swapped):
                parts.append(ref[pl.ds(64 * h + tile, 8, stride=8), :])
        for b, part in enumerate(exchange_groups(parts)):
            first_send[4 * tile + b] = part

    for load in loads[3:8]:
        load.wait()
    slab_high[...], slab_low[...] = split(inverse_ref[...])
    couple_high[...], couple_low[...] = split(coupling_ref[...])
    slab_map = (
        dot(slab_high[...], couple_high[...])
        + dot(slab_high[...], couple_low[...])
        + dot(slab_low[...], couple_high[...])
    )
    map_high, map_low = split(slab_map)
    index = lax.broadcasted_iota(jnp.int32, (orbitals, orbitals), 0)
    identity = (index == lanes_of((orbitals, orbitals))).astype(F32).astype(BF16)
    turned_high, turned_low = dot(identity, map_high, NT), dot(identity, map_low, NT)
    step_high[0], step_low[0] = turned_high.astype(BF16), turned_low.astype(BF16)
    turned = turned_high + turned_low
    steps[0, 0], steps[0, 1] = turned[:half], turned[half:]
    own_half = steps[0, core]
    for chunk in range(2):
        rest[0, chunk] = fold_rest(own_half[chunk_rows(chunk)])

    pl.semaphore_wait(barrier, peers - 1 + jnp.minimum(section, REACH) + jnp.minimum(sections - 1 - section, REACH))
    scatter_start(peers, me, first_send, first_recv, send_one, recv_one, as_is, mirrored)

    def rows_of(chunk):
        rows = chunk_rows(chunk)
        return pl.ds(rows.start, rows.stop - rows.start)

    def to_next(k, chunk):
        def copy(source, target, place):
            return pltpu.make_async_remote_copy(
                src_ref=source,
                dst_ref=target,
                send_sem=next_send.at[k - 1, chunk, place],
                recv_sem=next_recv.at[k - 1, chunk, place],
                device_id={"section": after},
                device_id_type=MESH,
            )

        whole = pl.ds(0, full)
        return (
            copy(steps.at[k - 1, core, rows_of(chunk), whole], inbox.at[k - 1, rows_of(chunk)], 0),
            copy(rest.at[k - 1, chunk], rest_in.at[k - 1, chunk], 1),
        )

    def to_twin(k, chunk):
        return pltpu.make_async_remote_copy(
            src_ref=steps.at[k - 1, core, rows_of(chunk)],
            dst_ref=steps.at[k - 1, core, rows_of(chunk)],
            send_sem=twin_send.at[k - 1, chunk],
            recv_sem=twin_recv.at[k - 1, chunk],
            device_id={"energy": twin},
            device_id_type=MESH,
        )

    def pass_on(k, chunk):
        @pl.when(has_after)
        def _():
            for copy in to_next(k, chunk):
                copy.start()

    def grow(k, chunk):
        @pl.when(has_before)
        def _():
            for copy in to_next(k - 1, chunk):
                copy.wait_recv()

        rows = rows_of(chunk)
        last = unfold_rest(rest_in[k - 2, chunk], rows.size)
        high, low = split(jnp.concatenate([inbox[k - 2, rows], last], axis=1))
        whole_high, whole_low = step_high[0], step_low[0]
        grown = dot(high, whole_high) + dot(low, whole_high) + dot(high, whole_low)
        steps[k - 1, core, rows] = grown
        if k < REACH:
            rest[k - 1, chunk] = fold_rest(grown)
            pass_on(k, chunk)
        to_twin(k, chunk).start()

    def gather(k):
        for chunk in range(2):
            to_twin(k, chunk).wait_recv()
        for part in range(2):
            rows = pl.ds(half * part, half)
            step_high[k - 1, rows], step_low[k - 1, rows] = split(steps[k - 1, part])

    @pl.when(jnp.logical_not(has_before))
    def _():
        inbox[...] = jnp.zeros_like(inbox)
        rest_in[...] = jnp.zeros_like(rest_in)

    for chunk in range(2):
        pass_on(1, chunk)

    pair_rows = rows_ref[...]
    for tile in range(8):
        index = lax.broadcasted_iota(jnp.int32, (orbitals, 128), 0)
        orbital_table[:, 128 * tile : 128 * tile + 128] = (
            (index == pair_rows[tile : tile + 1, :]).astype(F32).astype(BF16)
        )
    source = source_ref[...]
    base = product(jnp.broadcast_to(source, (16, orbitals)), slab_high[...], slab_low[...], NT)
    inverse_turned = dot(identity, slab_high[...], NT).astype(BF16), dot(identity, slab_low[...], NT).astype(BF16)
    lift_high[...], lift_low[...] = split(
        dot(inverse_turned[0], couple_high[...])
        + dot(inverse_turned[0], couple_low[...])
        + dot(inverse_turned[1], couple_high[...])
    )
    base_up = product(base, couple_high[...], couple_low[...], NN)
    grow(2, 0)

    for load in loads[8:13]:
        load.wait()
    wait_blocks(peers, first_recv, recv_one)

    first = first_recv[: peers // 2].reshape(peers * 4, 128)
    second = first_recv[peers // 2 :].reshape(peers * 4, 128)
    low_lanes = lanes_of(first.shape) < 64

    def parts_of(x):
        high = x.astype(BF16).astype(F32)
        low = x - high
        left = jnp.where(low_lanes, high, roll(low, 64))
        right = jnp.where(low_lanes, roll(high, 64), low)
        return jnp.concatenate([left, right], axis=0).astype(BF16)

    def forward(rows, x):
        halves = dot(fwd_high[rows], x) + dot(fwd_low[rows], x)
        return halves + roll(halves, 64)

    cosines, sines = pl.ds(0, HALF), pl.ds(HALF, HALF)
    cos_a, sin_a = forward(cosines, parts_of(first + second)), forward(sines, parts_of(first - second))
    spectrum[cosines], spectrum[sines] = cos_a, sin_a
    cos_b, sin_b = roll(cos_a, 96), roll(sin_a, 96)
    real, turned = cos_a * cos_b + sin_a * sin_b, sin_a * cos_b - cos_a * sin_b
    cos_half, sin_half = half_step[cosines], half_step[sines]
    even, odd = backward(
        inv_high, inv_low, real * cos_half - turned * sin_half, turned * cos_half + real * sin_half
    )
    group = lanes_of((peers * 2, 128)) // 32

    def join(polar):
        count = polar.shape[0] // 4
        joined = polar[:count]
        for q in range(1, 4):
            joined = jnp.where(group == q, roll(polar[count * q : count * (q + 1)], 32 * q), joined)
        return joined.reshape(peers // 2, 4, 128)

    second_send[: peers // 2] = join(even + odd)
    second_send[peers // 2 :] = join(even - odd)
    scatter_start(peers, me, second_send, second_recv, send_two, recv_two, mirrored, as_is)
    grow(2, 1)
    grow(3, 0)
    gather(2)
    grow(3, 1)
    gather(3)
    wait_blocks(peers, second_recv, recv_two)

    weighted = []
    for tile in range(8):
        lines = [second_recv[4 * tile + b] for b in range(4)]
        one, two = exchange_rows(jnp.concatenate(lines[:2], axis=0), jnp.concatenate(lines[2:], axis=0))
        weighted.append(jnp.concatenate([one, two], axis=0) * weight_ref[tile : tile + 1, :])
    both = dot(jnp.concatenate(split(jnp.concatenate(weighted, axis=1)), axis=0), orbital_table[...], NT)
    local_pol = both[:16] + both[16:]
    spread = local_pol * base
    upward[...] = base_up + product(spread, lift_high[...], lift_low[...], NN)

    def across(source, place, away):
        return pltpu.make_async_remote_copy(
            src_ref=source,
            dst_ref=arrived.at[place],
            send_sem=across_send.at[place],
            recv_sem=across_recv.at[place],
            device_id={"section": lax.rem(section + sections + away, sections)},
            device_id_type=MESH,
        )

    shift = across(upward, 0, -1)
    window = [across(offset, away, away) for away in range(1, REACH)]
    sweep = across(carried, REACH, REACH)

    @pl.when(has_before)
    def _():
        shift.start()

    guess = base + product(spread, slab_high[...], slab_low[...], NT)
    partial = product(source + local_pol * guess, slab_high[...], slab_low[...], NT)
    grow(4, 0)

    @pl.when(has_after)
    def _():
        shift.wait_recv()

    @pl.when(jnp.logical_not(has_after))
    def _():
        arrived[0] = jnp.zeros_like(upward)

    offset[...] = partial + product(arrived[0], slab_high[...], slab_low[...], NT)
    for away in range(1, REACH):

        @pl.when(section < sections - away)
        def _(away=away):
            window[away - 1].start()

    grow(4, 1)
    gather(4)
    carried[...] = offset[...]
    for away in range(1, REACH):

        @pl.when(section >= away)
        def _(away=away):
            window[away - 1].wait_recv()
            carried[...] += product(arrived[away], step_high[away - 1], step_low[away - 1], NN)

    @pl.when(section < REACH)
    def _():
        sweep.start()


    @pl.when(section >= REACH)
    def _():
        sweep.wait_recv()
        carried[...] += product(arrived[REACH], step_high[REACH - 1], step_low[REACH - 1], NN)

        @pl.when(section < sections - REACH)
        def _():
            sweep.start()

    screened = carried[...]
    both = dot(jnp.concatenate(split(screened), axis=0), orbital_table[...])
    pairs = both[:16] + both[16:]
    for tile in range(8):
        piece = pairs[:, 128 * tile : 128 * tile + 128] * weight_ref[tile : tile + 1, :]
        one, two = exchange_rows(piece[:8], piece[8:])
        for b, block in enumerate((one[:4], one[4:], two[:4], two[4:])):
            third_send[4 * tile + b] = block
    scatter_start(peers, me, third_send, values, send_three, recv_three, as_is, mirrored)

    for load in loads[13:]:
        load.wait()
    wait_blocks(peers, values, recv_three)
    convolve(
        values, spectrum, last_fwd_high, last_fwd_low, last_inv_high, last_inv_low, half_step, sigma_out
    )

    @pl.when(has_before)
    def _():
        shift.wait_send()

    for away in range(1, REACH):

        @pl.when(section < sections - away)
        def _(away=away):
            window[away - 1].wait_send()

    @pl.when(section < sections - REACH)
    def _():
        sweep.wait_send()

    for chunk in range(2):

        @pl.when(has_after)
        def _(chunk=chunk):
            for k in range(1, REACH):
                for copy in to_next(k, chunk):
                    copy.wait_send()

        for k in range(2, REACH + 1):
            to_twin(k, chunk).wait_send()

    wait_blocks(peers, first_send, send_one)
    wait_blocks(peers, second_send, send_two)
    wait_blocks(peers, third_send, send_three)


def on_device(peers, sections, g_less, g_greater, partner, pair_rows, pair_weight, source, slab_inverse, coupling):
    own, _, columns = g_less.shape
    energies = own * peers
    orbitals = slab_inverse.shape[-1]
    vmem = pl.BlockSpec(memory_space=pltpu.VMEM)
    hbm = pl.BlockSpec(memory_space=pltpu.HBM)
    square = (orbitals, orbitals)
    strip = (own, orbitals)
    sigma = pl.pallas_call(
        functools.partial(main_kernel, peers, sections),
        out_shape=pltpu.VMEM((columns // peers, energies), F32),
        in_specs=[hbm] * 17,
        out_specs=vmem,
        scratch_shapes=[
            pltpu.VMEM((128, 128), F32),
            pltpu.VMEM((128, 128), F32),
            pltpu.VMEM((8, 128), jnp.int32),
            pltpu.VMEM((8, 128), jnp.int32),
            pltpu.VMEM((8, 128), F32),
            pltpu.VMEM((1, orbitals), F32),
            pltpu.VMEM(square, F32),
            pltpu.VMEM(square, F32),
            pltpu.VMEM((LENGTH, energies // 2), BF16),
            pltpu.VMEM((LENGTH, energies // 2), BF16),
            pltpu.VMEM((energies, HALF), BF16),
            pltpu.VMEM((energies, HALF), BF16),
            pltpu.VMEM((LENGTH, 128), F32),
            pltpu.VMEM((LENGTH, energies // 2), BF16),
            pltpu.VMEM((LENGTH, energies // 2), BF16),
            pltpu.VMEM((energies, HALF), BF16),
            pltpu.VMEM((energies, HALF), BF16),
            pltpu.SemaphoreType.DMA((17,)),
            pltpu.VMEM((peers, 4, 128), F32),
            pltpu.VMEM((LENGTH, 128), F32),
            pltpu.VMEM((128, 128), F32),
            pltpu.VMEM((128, 128), F32),
            pltpu.VMEM((peers, 8, 128), F32),
            pltpu.VMEM((peers, 8, 128), F32),
            pltpu.VMEM((peers, 4, 128), F32),
            pltpu.VMEM((peers, 4, 128), F32),
            pltpu.VMEM((peers, 4, 128), F32),
            pltpu.VMEM((orbitals, columns), BF16),
            pltpu.VMEM(square, BF16),
            pltpu.VMEM(square, BF16),
            pltpu.VMEM(square, BF16),
            pltpu.VMEM(square, BF16),
            pltpu.VMEM(square, BF16),
            pltpu.VMEM(square, BF16),
            pltpu.VMEM((REACH, 2, orbitals // 2, orbitals), F32),
            pltpu.VMEM((REACH - 1, orbitals // 2, orbitals // 128 * 128), F32),
            pltpu.VMEM((REACH - 1, 2, 32, 128), F32),
            pltpu.VMEM((REACH - 1, 2, 32, 128), F32),
            pltpu.VMEM((REACH,) + square, BF16),
            pltpu.VMEM((REACH,) + square, BF16),
            pltpu.SemaphoreType.DMA((REACH, 2, 2)),
            pltpu.SemaphoreType.DMA((REACH, 2, 2)),
            pltpu.SemaphoreType.DMA((REACH, 2)),
            pltpu.SemaphoreType.DMA((REACH, 2)),
            pltpu.VMEM(strip, F32),
            pltpu.VMEM(strip, F32),
            pltpu.VMEM(strip, F32),
            pltpu.VMEM((REACH + 1,) + strip, F32),
            pltpu.SemaphoreType.DMA((REACH + 1,)),
            pltpu.SemaphoreType.DMA((REACH + 1,)),
        ]
        + [pltpu.SemaphoreType.DMA] * 6,
        compiler_params=pltpu.CompilerParams(
            collective_id=0, has_side_effects=True, vmem_limit_bytes=60 * 1024 * 1024
        ),
        name="update",
    )(
        g_less.reshape(-1, 128),
        g_greater.reshape(-1, 128),
        partner.reshape(-1, 128),
        pair_rows.reshape(-1, 128),
        pair_weight.reshape(-1, 128),
        source,
        slab_inverse[0],
        coupling[0],
        *forward_table(energy_order(peers, own, 2), energies),
        *inverse_table(energy_order(peers, own, 4), energies),
        half_steps(),
        *forward_table(energy_order(peers, own, 4), energies),
        *inverse_table(np.arange(energies // 2), energies),
    )
    return jnp.transpose(sigma)[:, None, :]


def solution(mesh):
    return jax.shard_map(
        functools.partial(on_device, mesh.shape["energy"], mesh.shape["section"]),
        mesh=mesh,
        in_specs=(
            P("energy", "section", None),
            P("energy", "section", None),
            P("section", None),
            P("section", None),
            P("section", None),
            P("section", None),
            P("section", None, None),
            P("section", None, None),
        ),
        out_specs=P(None, "section", "energy"),
        check_vma=False,
    )
```

```python
import functools
import math

import jax
import jax.numpy as jnp
import numpy as np
from jax import lax
from jax.experimental import pallas as pl
from jax.experimental.pallas import tpu as pltpu
from jax.sharding import PartitionSpec as P

MESH = pl.DeviceIdType.MESH
F32 = jnp.float32
BF16 = jnp.bfloat16
NT = (((1,), (1,)), ((), ()))
NN = (((1,), (0,)), ((), ()))
LENGTH = 768
HALF = LENGTH // 2
REACH = 4


def two_parts(table):
    table = np.asarray(table, np.float32)
    high = table.astype(jnp.bfloat16)
    low = (table - high.astype(np.float32)).astype(jnp.bfloat16)
    return jnp.asarray(high), jnp.asarray(low)


def angles(order, energies):
    times = np.asarray(order, np.float64) - (energies - 1) / 2
    return np.outer(np.arange(HALF) + 0.5, times) * (2.0 * math.pi / LENGTH)


def forward_table(order, energies):
    phase = angles(order, energies)
    return two_parts(np.concatenate([np.cos(phase), np.sin(phase)], axis=0))


def inverse_table(order, energies):
    phase = angles(order, energies).T
    scale = 2.0 / LENGTH / math.sqrt(energies)
    return two_parts(np.concatenate([np.cos(phase), np.sin(phase)], axis=0) * scale)


def half_steps():
    phase = (np.arange(HALF) + 0.5) * (math.pi / LENGTH)
    table = np.concatenate([np.cos(phase), np.sin(phase)])
    return jnp.asarray(np.broadcast_to(table[:, None], (LENGTH, 128)).astype(np.float32))


def energy_order(peers, own, fold):
    rows = own // fold
    group, sender, row = np.meshgrid(np.arange(fold), np.arange(peers // 2), np.arange(rows), indexing="ij")
    return (sender * own + group * rows + row).reshape(-1)


def lanes_of(shape):
    return lax.broadcasted_iota(jnp.int32, shape, len(shape) - 1)


def roll(x, shift, axis=1):
    return pltpu.roll(x, shift, axis)


def exchange_groups(parts):
    a0, a1, a2, a3 = parts
    lane = lanes_of(a0.shape)
    low = lane < 64
    near = lane % 64 < 32
    b0, b2 = jnp.where(low, a0, roll(a2, 64)), jnp.where(low, roll(a0, 64), a2)
    b1, b3 = jnp.where(low, a1, roll(a3, 64)), jnp.where(low, roll(a1, 64), a3)
    c0, c1 = jnp.where(near, b0, roll(b1, 32)), jnp.where(near, roll(b0, 96), b1)
    c2, c3 = jnp.where(near, b2, roll(b3, 32)), jnp.where(near, roll(b2, 96), b3)
    return c0, c1, c2, c3


def exchange_rows(first, second):
    lane = lanes_of(first.shape)
    row = lax.broadcasted_iota(jnp.int32, first.shape, 0)
    low = lane < 64
    upper_half = row < 4
    keep = (lane % 64 < 32) == upper_half
    one, two = jnp.where(low, first, roll(second, 64)), jnp.where(low, roll(first, 64), second)

    def inside(x):
        turned = roll(x, 4, 0)
        return jnp.where(keep, x, jnp.where(upper_half, roll(turned, 32), roll(turned, 96)))

    return inside(one), inside(two)


def split(x):
    high = x.astype(BF16)
    return high, (x - high.astype(F32)).astype(BF16)


def dot(x, y, dims=NN):
    return lax.dot_general(x, y, dims, preferred_element_type=F32)


def product(x, high, low, dims):
    rows = x.shape[0]
    x_high, x_low = split(x)
    both = dot(jnp.concatenate([x_high, x_low], axis=0), high, dims)
    return both[:rows] + both[rows:] + dot(x_high, low, dims)


def far_first(peers, n):
    return peers // 2 + (n + 1) // 2 * (1 - n % 2 * 2)


def scatter_start(peers, me, source, target, send, recv, source_place, target_place):
    mine = target_place(me)

    def one(n, _):
        peer = lax.rem(me + far_first(peers, n), peers)
        pltpu.make_async_remote_copy(
            src_ref=source.at[source_place(peer)],
            dst_ref=target.at[mine],
            send_sem=send,
            recv_sem=recv,
            device_id={"energy": peer},
            device_id_type=MESH,
        ).start()
        return 0

    lax.fori_loop(0, peers - 1, one, 0)
    target[mine] = source[source_place(me)]


def wait_blocks(peers, ref, semaphore):
    part = ref.at[pl.ds(0, peers - 1)]
    pltpu.make_async_copy(part, part, semaphore).wait()


def chunk_rows(chunk):
    return slice(0, 128) if chunk == 0 else slice(128, 208)


def fold_rest(rows):
    count, columns = rows.shape
    tail = rows[:, columns // 128 * 128 :]
    tail = jnp.concatenate([tail, jnp.zeros((count, 128 - tail.shape[1]), F32)], axis=1)
    if count < 128:
        tail = jnp.concatenate([tail, jnp.zeros((128 - count, 128), F32)], axis=0)
    group = lanes_of((32, 128)) // 32
    folded = tail[:32]
    for g in range(1, 4):
        folded = jnp.where(group == g, roll(tail[32 * g : 32 * g + 32], 32 * g), folded)
    return folded


def unfold_rest(folded, count):
    groups = [folded] + [roll(folded, 128 - 32 * g) for g in range(1, 4)]
    return jnp.concatenate(groups, axis=0)[:count, :32]


def backward(inv_high, inv_low, real, turned):
    def one(rows, x):
        high = x.astype(BF16).astype(F32)
        packed = jnp.where(lanes_of(x.shape) < 32, high, roll(x - high, 32)).astype(BF16)
        halves = dot(inv_high[rows], packed) + dot(inv_low[rows], packed)
        return halves + roll(halves, 96)

    count = inv_high.shape[0] // 2
    return one(pl.ds(0, count), real), one(pl.ds(count, count), turned)


def lane_take(x, index):
    return jnp.take_along_axis(x, index, axis=1, mode="promise_in_bounds")


def convolve(values_ref, spectrum_ref, fwd_high, fwd_low, inv_high, inv_low, half_step, sigma_ref):
    senders = values_ref.shape[0] // 2
    first = values_ref[:senders].reshape(senders * 4, 128)
    second = values_ref[senders:].reshape(senders * 4, 128)
    lane = lanes_of(first.shape)

    def parts_of(x):
        high = x.astype(BF16).astype(F32)
        low = x - high
        stacked = []
        for q in range(4):
            left = high if q == 0 else roll(high, 128 - 32 * q)
            right = low if q == 1 else roll(low, (160 - 32 * q) % 128)
            stacked.append(jnp.where(lane < 32, left, right))
        return jnp.concatenate(stacked, axis=0).astype(BF16)

    def forward(rows, x):
        halves = dot(fwd_high[rows], x) + dot(fwd_low[rows], x)
        return halves + roll(halves, 96)

    cosines, sines = pl.ds(0, HALF), pl.ds(HALF, HALF)
    cos_w, sin_w = forward(cosines, parts_of(first + second)), forward(sines, parts_of(first - second))
    cos_a, sin_a = spectrum_ref[cosines], spectrum_ref[sines]
    real, turned = cos_a * cos_w - sin_a * sin_w, cos_a * sin_w + sin_a * cos_w
    cos_half, sin_half = half_step[cosines], half_step[sines]
    even, odd = backward(
        inv_high, inv_low, real * cos_half + turned * sin_half, turned * cos_half - real * sin_half
    )
    count = even.shape[0]
    later = even - odd
    lane = lanes_of(later.shape)
    high = later.astype(BF16).astype(F32)
    middle = (later - high).astype(BF16).astype(F32)
    low = later - high - middle
    packed = jnp.where(lane < 32, high, jnp.where(lane < 64, roll(middle, 32), roll(low, 64))).astype(BF16)
    row = lax.broadcasted_iota(jnp.int32, (count, count), 0)
    reverse = (row + lanes_of((count, count)) == count - 1).astype(F32).astype(BF16)
    turned_round = dot(reverse, packed)
    later = turned_round + roll(turned_round, 96) + roll(turned_round, 64)
    sigma_ref[:, :count] = jnp.transpose(even + odd)[:32]
    sigma_ref[:, count:] = jnp.transpose(later)[:32]


def main_kernel(
    peers, sections,
    less_hbm, great_hbm, partner_hbm, rows_hbm, weight_hbm, source_hbm, inverse_hbm, coupling_hbm,
    fwd_high_hbm, fwd_low_hbm, inv_high_hbm, inv_low_hbm, step_hbm,
    last_fwd_high_hbm, last_fwd_low_hbm, last_inv_high_hbm, last_inv_low_hbm,
    sigma_out,
    less_ref, great_ref, partner_ref, rows_ref, weight_ref, source_ref, inverse_ref, coupling_ref,
    fwd_high, fwd_low, inv_high, inv_low, half_step,
    last_fwd_high, last_fwd_low, last_inv_high, last_inv_low, load_sem,
    values, spectrum,
    swapped, ordered, first_send, first_recv, second_send, second_recv, third_send,
    orbital_table, slab_high, slab_low, couple_high, couple_low, lift_high, lift_low,
    steps, inbox, rest, rest_in, step_high, step_low, next_send, next_recv, twin_send, twin_recv,
    upward, offset, carried, arrived, across_send, across_recv,
    send_one, recv_one, send_two, recv_two, send_three, recv_three,
):
    me = lax.axis_index("energy")
    section = lax.axis_index("section")
    has_before = section > 0
    has_after = section < sections - 1
    after = lax.rem(section + 1, sections)
    orbitals = inverse_ref.shape[0]
    half, full = orbitals // 2, orbitals // 128 * 128
    core = lax.rem(me, 2)
    in_upper = me >= peers // 2

    def as_is(place):
        return place

    def mirrored(place):
        return jnp.where(place < peers // 2, place, 3 * peers // 2 - 1 - place)

    twin = me + 1 - 2 * core

    barrier = pltpu.get_barrier_semaphore()

    def greet(n, _):
        peer = lax.rem(me + far_first(peers, n), peers)
        pl.semaphore_signal(barrier, inc=1, device_id={"energy": peer}, device_id_type=MESH)
        return 0

    lax.fori_loop(0, peers - 1, greet, 0)

    for away in range(1, REACH + 1):
        for there, other in ((section >= away, section - away), (section < sections - away, section + away)):

            @pl.when(there)
            def _(other=other):
                pl.semaphore_signal(barrier, inc=1, device_id={"section": other}, device_id_type=MESH)

    loads = [
        pltpu.make_async_copy(source, target, load_sem.at[place])
        for place, (source, target) in enumerate((
            (great_hbm, great_ref), (partner_hbm, partner_ref), (less_hbm, less_ref), (rows_hbm, rows_ref),
            (weight_hbm, weight_ref), (source_hbm, source_ref), (inverse_hbm, inverse_ref),
            (coupling_hbm, coupling_ref), (fwd_high_hbm, fwd_high), (fwd_low_hbm, fwd_low),
            (inv_high_hbm, inv_high), (inv_low_hbm, inv_low),
            (step_hbm, half_step),
            (last_fwd_high_hbm, last_fwd_high), (last_fwd_low_hbm, last_fwd_low),
            (last_inv_high_hbm, last_inv_high), (last_inv_low_hbm, last_inv_low),
        ))
    ]
    for load in loads:
        load.start()

    for load in loads[:3]:
        load.wait()

    partner = partner_ref[...]
    partner_tile, partner_lane = partner // 128, partner % 128
    for place in range(16):
        energy = pl.ds(pl.multiple_of(8 * jnp.where(in_upper, 15 - place, place), 8), 8)
        lines = great_ref[energy, :]
        total = jnp.zeros((8, 128), F32)
        for tile in range(8):
            line = jnp.broadcast_to(lines[tile : tile + 1, :], (8, 128))
            total = jnp.where(partner_tile == tile, lane_take(line, partner_lane), total)
        swapped[8 * place : 8 * place + 8, :] = total
        ordered[8 * place : 8 * place + 8, :] = less_ref[energy, :]

    for tile in range(8):
        parts = []
        for h in range(2):
            for ref in (ordered, swapped):
                parts.append(ref[pl.ds(64 * h + tile, 8, stride=8), :])
        for b, part in enumerate(exchange_groups(parts)):
            first_send[4 * tile + b] = part

    for load in loads[3:8]:
        load.wait()
    slab_high[...], slab_low[...] = split(inverse_ref[...])
    couple_high[...], couple_low[...] = split(coupling_ref[...])
    slab_map = (
        dot(slab_high[...], couple_high[...])
        + dot(slab_high[...], couple_low[...])
        + dot(slab_low[...], couple_high[...])
    )
    map_high, map_low = split(slab_map)
    index = lax.broadcasted_iota(jnp.int32, (orbitals, orbitals), 0)
    identity = (index == lanes_of((orbitals, orbitals))).astype(F32).astype(BF16)
    turned_high, turned_low = dot(identity, map_high, NT), dot(identity, map_low, NT)
    step_high[0], step_low[0] = turned_high.astype(BF16), turned_low.astype(BF16)
    turned = turned_high + turned_low
    steps[0, 0], steps[0, 1] = turned[:half], turned[half:]
    own_half = steps[0, core]
    for chunk in range(2):
        rest[0, chunk] = fold_rest(own_half[chunk_rows(chunk)])

    for away in range(1, REACH):

        @pl.when(section < away)
        def _(away=away):
            arrived[away] = jnp.zeros_like(arrived[away])

    pl.semaphore_wait(barrier, peers - 1 + jnp.minimum(section, REACH) + jnp.minimum(sections - 1 - section, REACH))
    scatter_start(peers, me, first_send, first_recv, send_one, recv_one, as_is, mirrored)

    def rows_of(chunk):
        rows = chunk_rows(chunk)
        return pl.ds(rows.start, rows.stop - rows.start)

    def to_next(k, chunk):
        def copy(source, target, place):
            return pltpu.make_async_remote_copy(
                src_ref=source,
                dst_ref=target,
                send_sem=next_send.at[k - 1, chunk, place],
                recv_sem=next_recv.at[k - 1, chunk, place],
                device_id={"section": after},
                device_id_type=MESH,
            )

        whole = pl.ds(0, full)
        return (
            copy(steps.at[k - 1, core, rows_of(chunk), whole], inbox.at[k - 1, rows_of(chunk)], 0),
            copy(rest.at[k - 1, chunk], rest_in.at[k - 1, chunk], 1),
        )

    def to_twin(k, chunk):
        return pltpu.make_async_remote_copy(
            src_ref=steps.at[k - 1, core, rows_of(chunk)],
            dst_ref=steps.at[k - 1, core, rows_of(chunk)],
            send_sem=twin_send.at[k - 1, chunk],
            recv_sem=twin_recv.at[k - 1, chunk],
            device_id={"energy": twin},
            device_id_type=MESH,
        )

    def pass_on(k, chunk):
        @pl.when(has_after)
        def _():
            for copy in to_next(k, chunk):
                copy.start()

    def grow(k, chunk):
        @pl.when(has_before)
        def _():
            for copy in to_next(k - 1, chunk):
                copy.wait_recv()

        rows = rows_of(chunk)
        last = unfold_rest(rest_in[k - 2, chunk], rows.size)
        high, low = split(jnp.concatenate([inbox[k - 2, rows], last], axis=1))
        whole_high, whole_low = step_high[0], step_low[0]
        grown = dot(high, whole_high) + dot(low, whole_high) + dot(high, whole_low)
        steps[k - 1, core, rows] = grown
        if k < REACH:
            rest[k - 1, chunk] = fold_rest(grown)
            pass_on(k, chunk)
        to_twin(k, chunk).start()

    def gather(k):
        for chunk in range(2):
            to_twin(k, chunk).wait_recv()
        for part in range(2):
            rows = pl.ds(half * part, half)
            step_high[k - 1, rows], step_low[k - 1, rows] = split(steps[k - 1, part])

    @pl.when(jnp.logical_not(has_before))
    def _():
        inbox[...] = jnp.zeros_like(inbox)
        rest_in[...] = jnp.zeros_like(rest_in)

    for chunk in range(2):
        pass_on(1, chunk)

    pair_rows = rows_ref[...]
    for tile in range(8):
        index = lax.broadcasted_iota(jnp.int32, (orbitals, 128), 0)
        orbital_table[:, 128 * tile : 128 * tile + 128] = (
            (index == pair_rows[tile : tile + 1, :]).astype(F32).astype(BF16)
        )
    source = source_ref[...]
    base = product(jnp.broadcast_to(source, (16, orbitals)), slab_high[...], slab_low[...], NT)
    inverse_turned = dot(identity, slab_high[...], NT).astype(BF16), dot(identity, slab_low[...], NT).astype(BF16)
    lift_high[...], lift_low[...] = split(
        dot(inverse_turned[0], couple_high[...])
        + dot(inverse_turned[0], couple_low[...])
        + dot(inverse_turned[1], couple_high[...])
    )
    base_up = product(base, couple_high[...], couple_low[...], NN)
    grow(2, 0)

    for load in loads[8:13]:
        load.wait()
    wait_blocks(peers, first_recv, recv_one)

    first = first_recv[: peers // 2].reshape(peers * 4, 128)
    second = first_recv[peers // 2 :].reshape(peers * 4, 128)
    low_lanes = lanes_of(first.shape) < 64

    def parts_of(x):
        high = x.astype(BF16).astype(F32)
        low = x - high
        left = jnp.where(low_lanes, high, roll(low, 64))
        right = jnp.where(low_lanes, roll(high, 64), low)
        return jnp.concatenate([left, right], axis=0).astype(BF16)

    def forward(rows, x):
        halves = dot(fwd_high[rows], x) + dot(fwd_low[rows], x)
        return halves + roll(halves, 64)

    cosines, sines = pl.ds(0, HALF), pl.ds(HALF, HALF)
    cos_a, sin_a = forward(cosines, parts_of(first + second)), forward(sines, parts_of(first - second))
    spectrum[cosines], spectrum[sines] = cos_a, sin_a
    cos_b, sin_b = roll(cos_a, 96), roll(sin_a, 96)
    real, turned = cos_a * cos_b + sin_a * sin_b, sin_a * cos_b - cos_a * sin_b
    cos_half, sin_half = half_step[cosines], half_step[sines]
    even, odd = backward(
        inv_high, inv_low, real * cos_half - turned * sin_half, turned * cos_half + real * sin_half
    )
    group = lanes_of((peers * 2, 128)) // 32

    def join(polar):
        count = polar.shape[0] // 4
        joined = polar[:count]
        for q in range(1, 4):
            joined = jnp.where(group == q, roll(polar[count * q : count * (q + 1)], 32 * q), joined)
        return joined.reshape(peers // 2, 4, 128)

    second_send[: peers // 2] = join(even + odd)
    second_send[peers // 2 :] = join(even - odd)
    scatter_start(peers, me, second_send, second_recv, send_two, recv_two, mirrored, as_is)
    grow(2, 1)
    grow(3, 0)
    gather(2)
    wait_blocks(peers, second_recv, recv_two)

    weighted = []
    for tile in range(8):
        lines = [second_recv[4 * tile + b] for b in range(4)]
        one, two = exchange_rows(jnp.concatenate(lines[:2], axis=0), jnp.concatenate(lines[2:], axis=0))
        weighted.append(jnp.concatenate([one, two], axis=0) * weight_ref[tile : tile + 1, :])
    both = dot(jnp.concatenate(split(jnp.concatenate(weighted, axis=1)), axis=0), orbital_table[...], NT)
    local_pol = both[:16] + both[16:]
    spread = local_pol * base
    upward[...] = base_up + product(spread, lift_high[...], lift_low[...], NN)

    def across(source, place, away):
        return pltpu.make_async_remote_copy(
            src_ref=source,
            dst_ref=arrived.at[place],
            send_sem=across_send.at[place],
            recv_sem=across_recv.at[place],
            device_id={"section": lax.rem(section + sections + away, sections)},
            device_id_type=MESH,
        )

    shift = across(upward, 0, -1)
    window = [across(offset, away, away) for away in range(1, REACH)]
    sweep = across(carried, REACH, REACH)

    @pl.when(has_before)
    def _():
        shift.start()

    grow(3, 1)
    guess = base + product(spread, slab_high[...], slab_low[...], NT)
    partial = product(source + local_pol * guess, slab_high[...], slab_low[...], NT)
    gather(3)
    grow(4, 0)

    @pl.when(has_after)
    def _():
        shift.wait_recv()

    @pl.when(jnp.logical_not(has_after))
    def _():
        arrived[0] = jnp.zeros_like(upward)

    offset[...] = partial + product(arrived[0], slab_high[...], slab_low[...], NT)
    for away in range(1, REACH):

        @pl.when(section < sections - away)
        def _(away=away):
            window[away - 1].start()

    grow(4, 1)
    gather(4)
    so_far = offset[...]
    for away in range(1, REACH):

        @pl.when(section >= away)
        def _(away=away):
            window[away - 1].wait_recv()

        if away != 2:
            for near in (1,) if away == 1 else (2, 3):
                so_far += product(arrived[near], step_high[near - 1], step_low[near - 1], NN)
    carried[...] = so_far

    @pl.when(section < REACH)
    def _():
        sweep.start()


    @pl.when(section >= REACH)
    def _():
        sweep.wait_recv()
        carried[...] += product(arrived[REACH], step_high[REACH - 1], step_low[REACH - 1], NN)

        @pl.when(section < sections - REACH)
        def _():
            sweep.start()

    screened = carried[...]
    both = dot(jnp.concatenate(split(screened), axis=0), orbital_table[...])
    pairs = both[:16] + both[16:]
    for tile in range(8):
        piece = pairs[:, 128 * tile : 128 * tile + 128] * weight_ref[tile : tile + 1, :]
        one, two = exchange_rows(piece[:8], piece[8:])
        for b, block in enumerate((one[:4], one[4:], two[:4], two[4:])):
            third_send[4 * tile + b] = block
    scatter_start(peers, me, third_send, values, send_three, recv_three, as_is, mirrored)

    for load in loads[13:]:
        load.wait()
    wait_blocks(peers, values, recv_three)
    convolve(
        values, spectrum, last_fwd_high, last_fwd_low, last_inv_high, last_inv_low, half_step, sigma_out
    )

    @pl.when(has_before)
    def _():
        shift.wait_send()

    for away in range(1, REACH):

        @pl.when(section < sections - away)
        def _(away=away):
            window[away - 1].wait_send()

    @pl.when(section < sections - REACH)
    def _():
        sweep.wait_send()

    for chunk in range(2):

        @pl.when(has_after)
        def _(chunk=chunk):
            for k in range(1, REACH):
                for copy in to_next(k, chunk):
                    copy.wait_send()

        for k in range(2, REACH + 1):
            to_twin(k, chunk).wait_send()

    wait_blocks(peers, first_send, send_one)
    wait_blocks(peers, second_send, send_two)
    wait_blocks(peers, third_send, send_three)


def on_device(peers, sections, g_less, g_greater, partner, pair_rows, pair_weight, source, slab_inverse, coupling):
    own, _, columns = g_less.shape
    energies = own * peers
    orbitals = slab_inverse.shape[-1]
    vmem = pl.BlockSpec(memory_space=pltpu.VMEM)
    hbm = pl.BlockSpec(memory_space=pltpu.HBM)
    square = (orbitals, orbitals)
    strip = (own, orbitals)
    sigma = pl.pallas_call(
        functools.partial(main_kernel, peers, sections),
        out_shape=pltpu.VMEM((columns // peers, energies), F32),
        in_specs=[hbm] * 17,
        out_specs=vmem,
        scratch_shapes=[
            pltpu.VMEM((128, 128), F32),
            pltpu.VMEM((128, 128), F32),
            pltpu.VMEM((8, 128), jnp.int32),
            pltpu.VMEM((8, 128), jnp.int32),
            pltpu.VMEM((8, 128), F32),
            pltpu.VMEM((1, orbitals), F32),
            pltpu.VMEM(square, F32),
            pltpu.VMEM(square, F32),
            pltpu.VMEM((LENGTH, energies // 2), BF16),
            pltpu.VMEM((LENGTH, energies // 2), BF16),
            pltpu.VMEM((energies, HALF), BF16),
            pltpu.VMEM((energies, HALF), BF16),
            pltpu.VMEM((LENGTH, 128), F32),
            pltpu.VMEM((LENGTH, energies // 2), BF16),
            pltpu.VMEM((LENGTH, energies // 2), BF16),
            pltpu.VMEM((energies, HALF), BF16),
            pltpu.VMEM((energies, HALF), BF16),
            pltpu.SemaphoreType.DMA((17,)),
            pltpu.VMEM((peers, 4, 128), F32),
            pltpu.VMEM((LENGTH, 128), F32),
            pltpu.VMEM((128, 128), F32),
            pltpu.VMEM((128, 128), F32),
            pltpu.VMEM((peers, 8, 128), F32),
            pltpu.VMEM((peers, 8, 128), F32),
            pltpu.VMEM((peers, 4, 128), F32),
            pltpu.VMEM((peers, 4, 128), F32),
            pltpu.VMEM((peers, 4, 128), F32),
            pltpu.VMEM((orbitals, columns), BF16),
            pltpu.VMEM(square, BF16),
            pltpu.VMEM(square, BF16),
            pltpu.VMEM(square, BF16),
            pltpu.VMEM(square, BF16),
            pltpu.VMEM(square, BF16),
            pltpu.VMEM(square, BF16),
            pltpu.VMEM((REACH, 2, orbitals // 2, orbitals), F32),
            pltpu.VMEM((REACH - 1, orbitals // 2, orbitals // 128 * 128), F32),
            pltpu.VMEM((REACH - 1, 2, 32, 128), F32),
            pltpu.VMEM((REACH - 1, 2, 32, 128), F32),
            pltpu.VMEM((REACH,) + square, BF16),
            pltpu.VMEM((REACH,) + square, BF16),
            pltpu.SemaphoreType.DMA((REACH, 2, 2)),
            pltpu.SemaphoreType.DMA((REACH, 2, 2)),
            pltpu.SemaphoreType.DMA((REACH, 2)),
            pltpu.SemaphoreType.DMA((REACH, 2)),
            pltpu.VMEM(strip, F32),
            pltpu.VMEM(strip, F32),
            pltpu.VMEM(strip, F32),
            pltpu.VMEM((REACH + 1,) + strip, F32),
            pltpu.SemaphoreType.DMA((REACH + 1,)),
            pltpu.SemaphoreType.DMA((REACH + 1,)),
        ]
        + [pltpu.SemaphoreType.DMA] * 6,
        compiler_params=pltpu.CompilerParams(
            collective_id=0, has_side_effects=True, vmem_limit_bytes=60 * 1024 * 1024
        ),
        name="update",
    )(
        g_less.reshape(-1, 128),
        g_greater.reshape(-1, 128),
        partner.reshape(-1, 128),
        pair_rows.reshape(-1, 128),
        pair_weight.reshape(-1, 128),
        source,
        slab_inverse[0],
        coupling[0],
        *forward_table(energy_order(peers, own, 2), energies),
        *inverse_table(energy_order(peers, own, 4), energies),
        half_steps(),
        *forward_table(energy_order(peers, own, 4), energies),
        *inverse_table(np.arange(energies // 2), energies),
    )
    return jnp.transpose(sigma)[:, None, :]


def solution(mesh):
    return jax.shard_map(
        functools.partial(on_device, mesh.shape["energy"], mesh.shape["section"]),
        mesh=mesh,
        in_specs=(
            P("energy", "section", None),
            P("energy", "section", None),
            P("section", None),
            P("section", None),
            P("section", None),
            P("section", None),
            P("section", None, None),
            P("section", None, None),
        ),
        out_specs=P(None, "section", "energy"),
        check_vma=False,
    )
```

```python
import functools
import math

import jax
import jax.numpy as jnp
import numpy as np
from jax import lax
from jax.experimental import pallas as pl
from jax.experimental.pallas import tpu as pltpu
from jax.sharding import PartitionSpec as P

MESH = pl.DeviceIdType.MESH
F32 = jnp.float32
BF16 = jnp.bfloat16
NT = (((1,), (1,)), ((), ()))
NN = (((1,), (0,)), ((), ()))
LENGTH = 768
HALF = LENGTH // 2
REACH = 4
CHUNKS = 3


def two_parts(table):
    table = np.asarray(table, np.float32)
    high = table.astype(jnp.bfloat16)
    low = (table - high.astype(np.float32)).astype(jnp.bfloat16)
    return jnp.asarray(high), jnp.asarray(low)


def angles(order, energies):
    times = np.asarray(order, np.float64) - (energies - 1) / 2
    return np.outer(np.arange(HALF) + 0.5, times) * (2.0 * math.pi / LENGTH)


def forward_table(order, energies):
    phase = angles(order, energies)
    return two_parts(np.concatenate([np.cos(phase), np.sin(phase)], axis=0))


def inverse_table(order, energies):
    phase = angles(order, energies).T
    scale = 2.0 / LENGTH / math.sqrt(energies)
    return two_parts(np.concatenate([np.cos(phase), np.sin(phase)], axis=0) * scale)


def half_steps():
    phase = (np.arange(HALF) + 0.5) * (math.pi / LENGTH)
    table = np.concatenate([np.cos(phase), np.sin(phase)])
    return jnp.asarray(np.broadcast_to(table[:, None], (LENGTH, 128)).astype(np.float32))


def energy_order(peers, own, fold):
    rows = own // fold
    group, sender, row = np.meshgrid(np.arange(fold), np.arange(peers // 2), np.arange(rows), indexing="ij")
    return (sender * own + group * rows + row).reshape(-1)


def lanes_of(shape):
    return lax.broadcasted_iota(jnp.int32, shape, len(shape) - 1)


def roll(x, shift, axis=1):
    return pltpu.roll(x, shift, axis)


def exchange_groups(parts):
    a0, a1, a2, a3 = parts
    lane = lanes_of(a0.shape)
    low = lane < 64
    near = lane % 64 < 32
    b0, b2 = jnp.where(low, a0, roll(a2, 64)), jnp.where(low, roll(a0, 64), a2)
    b1, b3 = jnp.where(low, a1, roll(a3, 64)), jnp.where(low, roll(a1, 64), a3)
    c0, c1 = jnp.where(near, b0, roll(b1, 32)), jnp.where(near, roll(b0, 96), b1)
    c2, c3 = jnp.where(near, b2, roll(b3, 32)), jnp.where(near, roll(b2, 96), b3)
    return c0, c1, c2, c3


def exchange_rows(first, second):
    lane = lanes_of(first.shape)
    row = lax.broadcasted_iota(jnp.int32, first.shape, 0)
    low = lane < 64
    upper_half = row < 4
    keep = (lane % 64 < 32) == upper_half
    one, two = jnp.where(low, first, roll(second, 64)), jnp.where(low, roll(first, 64), second)

    def inside(x):
        turned = roll(x, 4, 0)
        return jnp.where(keep, x, jnp.where(upper_half, roll(turned, 32), roll(turned, 96)))

    return inside(one), inside(two)


def split(x):
    high = x.astype(BF16)
    return high, (x - high.astype(F32)).astype(BF16)


def dot(x, y, dims=NN):
    return lax.dot_general(x, y, dims, preferred_element_type=F32)


def product(x, high, low, dims):
    rows = x.shape[0]
    x_high, x_low = split(x)
    both = dot(jnp.concatenate([x_high, x_low], axis=0), high, dims)
    return both[:rows] + both[rows:] + dot(x_high, low, dims)


def far_first(peers, n):
    return peers // 2 + (n + 1) // 2 * (1 - n % 2 * 2)


def scatter_start(peers, me, source, target, send, recv, source_place, target_place):
    mine = target_place(me)

    def one(n, _):
        peer = lax.rem(me + far_first(peers, n), peers)
        pltpu.make_async_remote_copy(
            src_ref=source.at[source_place(peer)],
            dst_ref=target.at[mine],
            send_sem=send,
            recv_sem=recv,
            device_id={"energy": peer},
            device_id_type=MESH,
        ).start()
        return 0

    lax.fori_loop(0, peers - 1, one, 0)
    target[mine] = source[source_place(me)]


def wait_blocks(peers, ref, semaphore):
    part = ref.at[pl.ds(0, peers - 1)]
    pltpu.make_async_copy(part, part, semaphore).wait()


def chunk_rows(chunk):
    edges = (0, 80, 144, 208)
    return slice(edges[chunk], edges[chunk + 1])


def fold_rest(rows):
    count, columns = rows.shape
    tail = rows[:, columns // 128 * 128 :]
    tail = jnp.concatenate([tail, jnp.zeros((count, 128 - tail.shape[1]), F32)], axis=1)
    if count < 128:
        tail = jnp.concatenate([tail, jnp.zeros((128 - count, 128), F32)], axis=0)
    group = lanes_of((32, 128)) // 32
    folded = tail[:32]
    for g in range(1, 4):
        folded = jnp.where(group == g, roll(tail[32 * g : 32 * g + 32], 32 * g), folded)
    return folded


def unfold_rest(folded, count):
    groups = [folded] + [roll(folded, 128 - 32 * g) for g in range(1, 4)]
    return jnp.concatenate(groups, axis=0)[:count, :32]


def backward(inv_high, inv_low, real, turned):
    def one(rows, x):
        high = x.astype(BF16).astype(F32)
        packed = jnp.where(lanes_of(x.shape) < 32, high, roll(x - high, 32)).astype(BF16)
        halves = dot(inv_high[rows], packed) + dot(inv_low[rows], packed)
        return halves + roll(halves, 96)

    count = inv_high.shape[0] // 2
    return one(pl.ds(0, count), real), one(pl.ds(count, count), turned)


def lane_take(x, index):
    return jnp.take_along_axis(x, index, axis=1, mode="promise_in_bounds")


def convolve(values_ref, spectrum_ref, fwd_high, fwd_low, inv_high, inv_low, half_step, sigma_ref):
    senders = values_ref.shape[0] // 2
    first = values_ref[:senders].reshape(senders * 4, 128)
    second = values_ref[senders:].reshape(senders * 4, 128)
    lane = lanes_of(first.shape)

    def parts_of(x):
        high = x.astype(BF16).astype(F32)
        low = x - high
        stacked = []
        for q in range(4):
            left = high if q == 0 else roll(high, 128 - 32 * q)
            right = low if q == 1 else roll(low, (160 - 32 * q) % 128)
            stacked.append(jnp.where(lane < 32, left, right))
        return jnp.concatenate(stacked, axis=0).astype(BF16)

    def forward(rows, x):
        halves = dot(fwd_high[rows], x) + dot(fwd_low[rows], x)
        return halves + roll(halves, 96)

    cosines, sines = pl.ds(0, HALF), pl.ds(HALF, HALF)
    cos_w, sin_w = forward(cosines, parts_of(first + second)), forward(sines, parts_of(first - second))
    cos_a, sin_a = spectrum_ref[cosines], spectrum_ref[sines]
    real, turned = cos_a * cos_w - sin_a * sin_w, cos_a * sin_w + sin_a * cos_w
    cos_half, sin_half = half_step[cosines], half_step[sines]
    even, odd = backward(
        inv_high, inv_low, real * cos_half + turned * sin_half, turned * cos_half - real * sin_half
    )
    count = even.shape[0]
    later = even - odd
    lane = lanes_of(later.shape)
    high = later.astype(BF16).astype(F32)
    middle = (later - high).astype(BF16).astype(F32)
    low = later - high - middle
    packed = jnp.where(lane < 32, high, jnp.where(lane < 64, roll(middle, 32), roll(low, 64))).astype(BF16)
    row = lax.broadcasted_iota(jnp.int32, (count, count), 0)
    reverse = (row + lanes_of((count, count)) == count - 1).astype(F32).astype(BF16)
    turned_round = dot(reverse, packed)
    later = turned_round + roll(turned_round, 96) + roll(turned_round, 64)
    sigma_ref[:, :count] = jnp.transpose(even + odd)[:32]
    sigma_ref[:, count:] = jnp.transpose(later)[:32]


def main_kernel(
    peers, sections,
    less_hbm, great_hbm, partner_hbm, rows_hbm, weight_hbm, source_hbm, inverse_hbm, coupling_hbm,
    fwd_high_hbm, fwd_low_hbm, inv_high_hbm, inv_low_hbm, step_hbm,
    last_fwd_high_hbm, last_fwd_low_hbm, last_inv_high_hbm, last_inv_low_hbm,
    sigma_out,
    less_ref, great_ref, partner_ref, rows_ref, weight_ref, source_ref, inverse_ref, coupling_ref,
    fwd_high, fwd_low, inv_high, inv_low, half_step,
    last_fwd_high, last_fwd_low, last_inv_high, last_inv_low, load_sem,
    values, spectrum,
    swapped, ordered, first_send, first_recv, second_send, second_recv, third_send,
    orbital_table, slab_high, slab_low, couple_high, couple_low, lift_high, lift_low,
    steps, inbox, rest, rest_in, step_high, step_low, next_send, next_recv, twin_send, twin_recv,
    upward, offset, carried, arrived, across_send, across_recv,
    send_one, recv_one, send_two, recv_two, send_three, recv_three,
):
    me = lax.axis_index("energy")
    section = lax.axis_index("section")
    has_before = section > 0
    has_after = section < sections - 1
    after = lax.rem(section + 1, sections)
    orbitals = inverse_ref.shape[0]
    half, full = orbitals // 2, orbitals // 128 * 128
    core = lax.rem(me, 2)
    in_upper = me >= peers // 2

    def as_is(place):
        return place

    def mirrored(place):
        return jnp.where(place < peers // 2, place, 3 * peers // 2 - 1 - place)

    twin = me + 1 - 2 * core

    barrier = pltpu.get_barrier_semaphore()

    def greet(n, _):
        peer = lax.rem(me + far_first(peers, n), peers)
        pl.semaphore_signal(barrier, inc=1, device_id={"energy": peer}, device_id_type=MESH)
        return 0

    lax.fori_loop(0, peers - 1, greet, 0)

    for away in range(1, REACH + 1):
        for there, other in ((section >= away, section - away), (section < sections - away, section + away)):

            @pl.when(there)
            def _(other=other):
                pl.semaphore_signal(barrier, inc=1, device_id={"section": other}, device_id_type=MESH)

    loads = [
        pltpu.make_async_copy(source, target, load_sem.at[place])
        for place, (source, target) in enumerate((
            (great_hbm, great_ref), (partner_hbm, partner_ref), (less_hbm, less_ref), (rows_hbm, rows_ref),
            (weight_hbm, weight_ref), (source_hbm, source_ref), (inverse_hbm, inverse_ref),
            (coupling_hbm, coupling_ref), (fwd_high_hbm, fwd_high), (fwd_low_hbm, fwd_low),
            (inv_high_hbm, inv_high), (inv_low_hbm, inv_low),
            (step_hbm, half_step),
            (last_fwd_high_hbm, last_fwd_high), (last_fwd_low_hbm, last_fwd_low),
            (last_inv_high_hbm, last_inv_high), (last_inv_low_hbm, last_inv_low),
        ))
    ]
    for load in loads:
        load.start()

    for load in loads[:3]:
        load.wait()

    partner = partner_ref[...]
    partner_tile, partner_lane = partner // 128, partner % 128
    for place in range(16):
        energy = pl.ds(pl.multiple_of(8 * jnp.where(in_upper, 15 - place, place), 8), 8)
        lines = great_ref[energy, :]
        total = jnp.zeros((8, 128), F32)
        for tile in range(8):
            line = jnp.broadcast_to(lines[tile : tile + 1, :], (8, 128))
            total = jnp.where(partner_tile == tile, lane_take(line, partner_lane), total)
        swapped[8 * place : 8 * place + 8, :] = total
        ordered[8 * place : 8 * place + 8, :] = less_ref[energy, :]

    for tile in range(8):
        parts = []
        for h in range(2):
            for ref in (ordered, swapped):
                parts.append(ref[pl.ds(64 * h + tile, 8, stride=8), :])
        for b, part in enumerate(exchange_groups(parts)):
            first_send[4 * tile + b] = part

    for load in loads[3:8]:
        load.wait()
    slab_high[...], slab_low[...] = split(inverse_ref[...])
    couple_high[...], couple_low[...] = split(coupling_ref[...])
    slab_map = (
        dot(slab_high[...], couple_high[...])
        + dot(slab_high[...], couple_low[...])
        + dot(slab_low[...], couple_high[...])
    )
    map_high, map_low = split(slab_map)
    index = lax.broadcasted_iota(jnp.int32, (orbitals, orbitals), 0)
    identity = (index == lanes_of((orbitals, orbitals))).astype(F32).astype(BF16)
    turned_high, turned_low = dot(identity, map_high, NT), dot(identity, map_low, NT)
    step_high[0], step_low[0] = turned_high.astype(BF16), turned_low.astype(BF16)
    turned = turned_high + turned_low
    steps[0, 0], steps[0, 1] = turned[:half], turned[half:]
    own_half = steps[0, core]
    for chunk in range(CHUNKS):
        rest[0, chunk] = fold_rest(own_half[chunk_rows(chunk)])

    for away in range(1, REACH):

        @pl.when(section < away)
        def _(away=away):
            arrived[away] = jnp.zeros_like(arrived[away])

    pl.semaphore_wait(barrier, peers - 1 + jnp.minimum(section, REACH) + jnp.minimum(sections - 1 - section, REACH))
    scatter_start(peers, me, first_send, first_recv, send_one, recv_one, as_is, mirrored)

    def rows_of(chunk):
        rows = chunk_rows(chunk)
        return pl.ds(rows.start, rows.stop - rows.start)

    def to_next(k, chunk):
        def copy(source, target, place):
            return pltpu.make_async_remote_copy(
                src_ref=source,
                dst_ref=target,
                send_sem=next_send.at[k - 1, chunk, place],
                recv_sem=next_recv.at[k - 1, chunk, place],
                device_id={"section": after},
                device_id_type=MESH,
            )

        whole = pl.ds(0, full)
        return (
            copy(steps.at[k - 1, core, rows_of(chunk), whole], inbox.at[k - 1, rows_of(chunk)], 0),
            copy(rest.at[k - 1, chunk], rest_in.at[k - 1, chunk], 1),
        )

    def to_twin(k, chunk):
        return pltpu.make_async_remote_copy(
            src_ref=steps.at[k - 1, core, rows_of(chunk)],
            dst_ref=steps.at[k - 1, core, rows_of(chunk)],
            send_sem=twin_send.at[k - 1, chunk],
            recv_sem=twin_recv.at[k - 1, chunk],
            device_id={"energy": twin},
            device_id_type=MESH,
        )

    def pass_on(k, chunk):
        @pl.when(has_after)
        def _():
            for copy in to_next(k, chunk):
                copy.start()

    def grow(k, chunk):
        @pl.when(has_before)
        def _():
            for copy in to_next(k - 1, chunk):
                copy.wait_recv()

        rows = rows_of(chunk)
        last = unfold_rest(rest_in[k - 2, chunk], rows.size)
        high, low = split(jnp.concatenate([inbox[k - 2, rows], last], axis=1))
        whole_high, whole_low = step_high[0], step_low[0]
        grown = dot(high, whole_high) + dot(low, whole_high) + dot(high, whole_low)
        steps[k - 1, core, rows] = grown
        if k < REACH:
            rest[k - 1, chunk] = fold_rest(grown)
            pass_on(k, chunk)
        to_twin(k, chunk).start()

    def gather(k):
        for chunk in range(CHUNKS):
            to_twin(k, chunk).wait_recv()
        for part in range(2):
            rows = pl.ds(half * part, half)
            step_high[k - 1, rows], step_low[k - 1, rows] = split(steps[k - 1, part])

    @pl.when(jnp.logical_not(has_before))
    def _():
        inbox[...] = jnp.zeros_like(inbox)
        rest_in[...] = jnp.zeros_like(rest_in)

    for chunk in range(CHUNKS):
        pass_on(1, chunk)

    pair_rows = rows_ref[...]
    for tile in range(8):
        index = lax.broadcasted_iota(jnp.int32, (orbitals, 128), 0)
        orbital_table[:, 128 * tile : 128 * tile + 128] = (
            (index == pair_rows[tile : tile + 1, :]).astype(F32).astype(BF16)
        )
    source = source_ref[...]
    base = product(jnp.broadcast_to(source, (16, orbitals)), slab_high[...], slab_low[...], NT)
    inverse_turned = dot(identity, slab_high[...], NT).astype(BF16), dot(identity, slab_low[...], NT).astype(BF16)
    lift_high[...], lift_low[...] = split(
        dot(inverse_turned[0], couple_high[...])
        + dot(inverse_turned[0], couple_low[...])
        + dot(inverse_turned[1], couple_high[...])
    )
    base_up = product(base, couple_high[...], couple_low[...], NN)
    grow(2, 0)

    for load in loads[8:13]:
        load.wait()
    wait_blocks(peers, first_recv, recv_one)

    first = first_recv[: peers // 2].reshape(peers * 4, 128)
    second = first_recv[peers // 2 :].reshape(peers * 4, 128)
    low_lanes = lanes_of(first.shape) < 64

    def parts_of(x):
        high = x.astype(BF16).astype(F32)
        low = x - high
        left = jnp.where(low_lanes, high, roll(low, 64))
        right = jnp.where(low_lanes, roll(high, 64), low)
        return jnp.concatenate([left, right], axis=0).astype(BF16)

    def forward(rows, x):
        halves = dot(fwd_high[rows], x) + dot(fwd_low[rows], x)
        return halves + roll(halves, 64)

    cosines, sines = pl.ds(0, HALF), pl.ds(HALF, HALF)
    cos_a, sin_a = forward(cosines, parts_of(first + second)), forward(sines, parts_of(first - second))
    spectrum[cosines], spectrum[sines] = cos_a, sin_a
    cos_b, sin_b = roll(cos_a, 96), roll(sin_a, 96)
    real, turned = cos_a * cos_b + sin_a * sin_b, sin_a * cos_b - cos_a * sin_b
    cos_half, sin_half = half_step[cosines], half_step[sines]
    even, odd = backward(
        inv_high, inv_low, real * cos_half - turned * sin_half, turned * cos_half + real * sin_half
    )
    group = lanes_of((peers * 2, 128)) // 32

    def join(polar):
        count = polar.shape[0] // 4
        joined = polar[:count]
        for q in range(1, 4):
            joined = jnp.where(group == q, roll(polar[count * q : count * (q + 1)], 32 * q), joined)
        return joined.reshape(peers // 2, 4, 128)

    second_send[: peers // 2] = join(even + odd)
    second_send[peers // 2 :] = join(even - odd)
    scatter_start(peers, me, second_send, second_recv, send_two, recv_two, mirrored, as_is)
    grow(2, 1)
    grow(2, 2)
    grow(3, 0)
    grow(3, 1)
    gather(2)
    wait_blocks(peers, second_recv, recv_two)

    weighted = []
    for tile in range(8):
        lines = [second_recv[4 * tile + b] for b in range(4)]
        one, two = exchange_rows(jnp.concatenate(lines[:2], axis=0), jnp.concatenate(lines[2:], axis=0))
        weighted.append(jnp.concatenate([one, two], axis=0) * weight_ref[tile : tile + 1, :])
    both = dot(jnp.concatenate(split(jnp.concatenate(weighted, axis=1)), axis=0), orbital_table[...], NT)
    local_pol = both[:16] + both[16:]
    spread = local_pol * base
    upward[...] = base_up + product(spread, lift_high[...], lift_low[...], NN)

    def across(source, place, away):
        return pltpu.make_async_remote_copy(
            src_ref=source,
            dst_ref=arrived.at[place],
            send_sem=across_send.at[place],
            recv_sem=across_recv.at[place],
            device_id={"section": lax.rem(section + sections + away, sections)},
            device_id_type=MESH,
        )

    shift = across(upward, 0, -1)
    window = [across(offset, away, away) for away in range(1, REACH)]
    sweep = across(carried, REACH, REACH)

    @pl.when(has_before)
    def _():
        shift.start()

    grow(3, 2)
    guess = base + product(spread, slab_high[...], slab_low[...], NT)
    partial = product(source + local_pol * guess, slab_high[...], slab_low[...], NT)
    gather(3)
    grow(4, 0)

    @pl.when(has_after)
    def _():
        shift.wait_recv()

    @pl.when(jnp.logical_not(has_after))
    def _():
        arrived[0] = jnp.zeros_like(upward)

    offset[...] = partial + product(arrived[0], slab_high[...], slab_low[...], NT)
    for away in range(1, REACH):

        @pl.when(section < sections - away)
        def _(away=away):
            window[away - 1].start()

    grow(4, 1)
    grow(4, 2)
    gather(4)
    so_far = offset[...]
    for away in range(1, REACH):

        @pl.when(section >= away)
        def _(away=away):
            window[away - 1].wait_recv()

        if away != 2:
            for near in (1,) if away == 1 else (2, 3):
                so_far += product(arrived[near], step_high[near - 1], step_low[near - 1], NN)
    carried[...] = so_far

    @pl.when(section < REACH)
    def _():
        sweep.start()


    @pl.when(section >= REACH)
    def _():
        sweep.wait_recv()
        carried[...] += product(arrived[REACH], step_high[REACH - 1], step_low[REACH - 1], NN)

        @pl.when(section < sections - REACH)
        def _():
            sweep.start()

    screened = carried[...]
    both = dot(jnp.concatenate(split(screened), axis=0), orbital_table[...])
    pairs = both[:16] + both[16:]
    for tile in range(8):
        piece = pairs[:, 128 * tile : 128 * tile + 128] * weight_ref[tile : tile + 1, :]
        one, two = exchange_rows(piece[:8], piece[8:])
        for b, block in enumerate((one[:4], one[4:], two[:4], two[4:])):
            third_send[4 * tile + b] = block
    scatter_start(peers, me, third_send, values, send_three, recv_three, as_is, mirrored)

    for load in loads[13:]:
        load.wait()
    wait_blocks(peers, values, recv_three)
    convolve(
        values, spectrum, last_fwd_high, last_fwd_low, last_inv_high, last_inv_low, half_step, sigma_out
    )

    @pl.when(has_before)
    def _():
        shift.wait_send()

    for away in range(1, REACH):

        @pl.when(section < sections - away)
        def _(away=away):
            window[away - 1].wait_send()

    @pl.when(section < sections - REACH)
    def _():
        sweep.wait_send()

    for chunk in range(CHUNKS):

        @pl.when(has_after)
        def _(chunk=chunk):
            for k in range(1, REACH):
                for copy in to_next(k, chunk):
                    copy.wait_send()

        for k in range(2, REACH + 1):
            to_twin(k, chunk).wait_send()

    wait_blocks(peers, first_send, send_one)
    wait_blocks(peers, second_send, send_two)
    wait_blocks(peers, third_send, send_three)


def on_device(peers, sections, g_less, g_greater, partner, pair_rows, pair_weight, source, slab_inverse, coupling):
    own, _, columns = g_less.shape
    energies = own * peers
    orbitals = slab_inverse.shape[-1]
    vmem = pl.BlockSpec(memory_space=pltpu.VMEM)
    hbm = pl.BlockSpec(memory_space=pltpu.HBM)
    square = (orbitals, orbitals)
    strip = (own, orbitals)
    sigma = pl.pallas_call(
        functools.partial(main_kernel, peers, sections),
        out_shape=pltpu.VMEM((columns // peers, energies), F32),
        in_specs=[hbm] * 17,
        out_specs=vmem,
        scratch_shapes=[
            pltpu.VMEM((128, 128), F32),
            pltpu.VMEM((128, 128), F32),
            pltpu.VMEM((8, 128), jnp.int32),
            pltpu.VMEM((8, 128), jnp.int32),
            pltpu.VMEM((8, 128), F32),
            pltpu.VMEM((1, orbitals), F32),
            pltpu.VMEM(square, F32),
            pltpu.VMEM(square, F32),
            pltpu.VMEM((LENGTH, energies // 2), BF16),
            pltpu.VMEM((LENGTH, energies // 2), BF16),
            pltpu.VMEM((energies, HALF), BF16),
            pltpu.VMEM((energies, HALF), BF16),
            pltpu.VMEM((LENGTH, 128), F32),
            pltpu.VMEM((LENGTH, energies // 2), BF16),
            pltpu.VMEM((LENGTH, energies // 2), BF16),
            pltpu.VMEM((energies, HALF), BF16),
            pltpu.VMEM((energies, HALF), BF16),
            pltpu.SemaphoreType.DMA((17,)),
            pltpu.VMEM((peers, 4, 128), F32),
            pltpu.VMEM((LENGTH, 128), F32),
            pltpu.VMEM((128, 128), F32),
            pltpu.VMEM((128, 128), F32),
            pltpu.VMEM((peers, 8, 128), F32),
            pltpu.VMEM((peers, 8, 128), F32),
            pltpu.VMEM((peers, 4, 128), F32),
            pltpu.VMEM((peers, 4, 128), F32),
            pltpu.VMEM((peers, 4, 128), F32),
            pltpu.VMEM((orbitals, columns), BF16),
            pltpu.VMEM(square, BF16),
            pltpu.VMEM(square, BF16),
            pltpu.VMEM(square, BF16),
            pltpu.VMEM(square, BF16),
            pltpu.VMEM(square, BF16),
            pltpu.VMEM(square, BF16),
            pltpu.VMEM((REACH, 2, orbitals // 2, orbitals), F32),
            pltpu.VMEM((REACH - 1, orbitals // 2, orbitals // 128 * 128), F32),
            pltpu.VMEM((REACH - 1, CHUNKS, 32, 128), F32),
            pltpu.VMEM((REACH - 1, CHUNKS, 32, 128), F32),
            pltpu.VMEM((REACH,) + square, BF16),
            pltpu.VMEM((REACH,) + square, BF16),
            pltpu.SemaphoreType.DMA((REACH, CHUNKS, 2)),
            pltpu.SemaphoreType.DMA((REACH, CHUNKS, 2)),
            pltpu.SemaphoreType.DMA((REACH, CHUNKS)),
            pltpu.SemaphoreType.DMA((REACH, CHUNKS)),
            pltpu.VMEM(strip, F32),
            pltpu.VMEM(strip, F32),
            pltpu.VMEM(strip, F32),
            pltpu.VMEM((REACH + 1,) + strip, F32),
            pltpu.SemaphoreType.DMA((REACH + 1,)),
            pltpu.SemaphoreType.DMA((REACH + 1,)),
        ]
        + [pltpu.SemaphoreType.DMA] * 6,
        compiler_params=pltpu.CompilerParams(
            collective_id=0, has_side_effects=True, vmem_limit_bytes=60 * 1024 * 1024
        ),
        name="update",
    )(
        g_less.reshape(-1, 128),
        g_greater.reshape(-1, 128),
        partner.reshape(-1, 128),
        pair_rows.reshape(-1, 128),
        pair_weight.reshape(-1, 128),
        source,
        slab_inverse[0],
        coupling[0],
        *forward_table(energy_order(peers, own, 2), energies),
        *inverse_table(energy_order(peers, own, 4), energies),
        half_steps(),
        *forward_table(energy_order(peers, own, 4), energies),
        *inverse_table(np.arange(energies // 2), energies),
    )
    return jnp.transpose(sigma)[:, None, :]


def solution(mesh):
    return jax.shard_map(
        functools.partial(on_device, mesh.shape["energy"], mesh.shape["section"]),
        mesh=mesh,
        in_specs=(
            P("energy", "section", None),
            P("energy", "section", None),
            P("section", None),
            P("section", None),
            P("section", None),
            P("section", None),
            P("section", None, None),
            P("section", None, None),
        ),
        out_specs=P(None, "section", "energy"),
        check_vma=False,
    )
```

```python
import functools
import math

import jax
import jax.numpy as jnp
import numpy as np
from jax import lax
from jax.experimental import pallas as pl
from jax.experimental.pallas import tpu as pltpu
from jax.sharding import PartitionSpec as P

MESH = pl.DeviceIdType.MESH
F32 = jnp.float32
BF16 = jnp.bfloat16
NT = (((1,), (1,)), ((), ()))
NN = (((1,), (0,)), ((), ()))
LENGTH = 768
HALF = LENGTH // 2
REACH = 4


def two_parts(table):
    table = np.asarray(table, np.float32)
    high = table.astype(jnp.bfloat16)
    low = (table - high.astype(np.float32)).astype(jnp.bfloat16)
    return jnp.asarray(high), jnp.asarray(low)


def angles(order, energies):
    times = np.asarray(order, np.float64) - (energies - 1) / 2
    return np.outer(np.arange(HALF) + 0.5, times) * (2.0 * math.pi / LENGTH)


def forward_table(order, energies):
    phase = angles(order, energies)
    return two_parts(np.concatenate([np.cos(phase), np.sin(phase)], axis=0))


def inverse_table(order, energies):
    phase = angles(order, energies).T
    scale = 2.0 / LENGTH / math.sqrt(energies)
    return two_parts(np.concatenate([np.cos(phase), np.sin(phase)], axis=0) * scale)


def half_steps():
    phase = (np.arange(HALF) + 0.5) * (math.pi / LENGTH)
    table = np.concatenate([np.cos(phase), np.sin(phase)])
    return jnp.asarray(np.broadcast_to(table[:, None], (LENGTH, 128)).astype(np.float32))


def energy_order(peers, own, fold):
    rows = own // fold
    group, sender, row = np.meshgrid(np.arange(fold), np.arange(peers // 2), np.arange(rows), indexing="ij")
    return (sender * own + group * rows + row).reshape(-1)


def lanes_of(shape):
    return lax.broadcasted_iota(jnp.int32, shape, len(shape) - 1)


def roll(x, shift, axis=1):
    return pltpu.roll(x, shift, axis)


def exchange_groups(parts):
    a0, a1, a2, a3 = parts
    lane = lanes_of(a0.shape)
    low = lane < 64
    near = lane % 64 < 32
    b0, b2 = jnp.where(low, a0, roll(a2, 64)), jnp.where(low, roll(a0, 64), a2)
    b1, b3 = jnp.where(low, a1, roll(a3, 64)), jnp.where(low, roll(a1, 64), a3)
    c0, c1 = jnp.where(near, b0, roll(b1, 32)), jnp.where(near, roll(b0, 96), b1)
    c2, c3 = jnp.where(near, b2, roll(b3, 32)), jnp.where(near, roll(b2, 96), b3)
    return c0, c1, c2, c3


def exchange_rows(first, second):
    lane = lanes_of(first.shape)
    row = lax.broadcasted_iota(jnp.int32, first.shape, 0)
    low = lane < 64
    upper_half = row < 4
    keep = (lane % 64 < 32) == upper_half
    one, two = jnp.where(low, first, roll(second, 64)), jnp.where(low, roll(first, 64), second)

    def inside(x):
        turned = roll(x, 4, 0)
        return jnp.where(keep, x, jnp.where(upper_half, roll(turned, 32), roll(turned, 96)))

    return inside(one), inside(two)


def split(x):
    high = x.astype(BF16)
    return high, (x - high.astype(F32)).astype(BF16)


def dot(x, y, dims=NN):
    return lax.dot_general(x, y, dims, preferred_element_type=F32)


def product(x, high, low, dims):
    rows = x.shape[0]
    x_high, x_low = split(x)
    both = dot(jnp.concatenate([x_high, x_low], axis=0), high, dims)
    return both[:rows] + both[rows:] + dot(x_high, low, dims)


def far_first(peers, n):
    return peers // 2 + (n + 1) // 2 * (1 - n % 2 * 2)


def scatter_start(peers, me, source, target, send, recv, source_place, target_place):
    mine = target_place(me)

    def one(n, _):
        peer = lax.rem(me + far_first(peers, n), peers)
        pltpu.make_async_remote_copy(
            src_ref=source.at[source_place(peer)],
            dst_ref=target.at[mine],
            send_sem=send,
            recv_sem=recv,
            device_id={"energy": peer},
            device_id_type=MESH,
        ).start()
        return 0

    lax.fori_loop(0, peers - 1, one, 0)
    target[mine] = source[source_place(me)]


def wait_blocks(peers, ref, semaphore):
    part = ref.at[pl.ds(0, peers - 1)]
    pltpu.make_async_copy(part, part, semaphore).wait()


def chunk_rows(chunk):
    return slice(0, 128) if chunk == 0 else slice(128, 208)


def fold_rest(rows):
    count, columns = rows.shape
    tail = rows[:, columns // 128 * 128 :]
    tail = jnp.concatenate([tail, jnp.zeros((count, 128 - tail.shape[1]), F32)], axis=1)
    if count < 128:
        tail = jnp.concatenate([tail, jnp.zeros((128 - count, 128), F32)], axis=0)
    group = lanes_of((32, 128)) // 32
    folded = tail[:32]
    for g in range(1, 4):
        folded = jnp.where(group == g, roll(tail[32 * g : 32 * g + 32], 32 * g), folded)
    return folded


def unfold_rest(folded, count):
    groups = [folded] + [roll(folded, 128 - 32 * g) for g in range(1, 4)]
    return jnp.concatenate(groups, axis=0)[:count, :32]


def backward(inv_high, inv_low, real, turned):
    def one(rows, x):
        high = x.astype(BF16).astype(F32)
        packed = jnp.where(lanes_of(x.shape) < 32, high, roll(x - high, 32)).astype(BF16)
        halves = dot(inv_high[rows], packed) + dot(inv_low[rows], packed)
        return halves + roll(halves, 96)

    count = inv_high.shape[0] // 2
    return one(pl.ds(0, count), real), one(pl.ds(count, count), turned)


def lane_take(x, index):
    return jnp.take_along_axis(x, index, axis=1, mode="promise_in_bounds")


def convolve(values_ref, spectrum_ref, fwd_high, fwd_low, inv_high, inv_low, half_step, sigma_ref):
    senders = values_ref.shape[0] // 2
    first = values_ref[:senders].reshape(senders * 4, 128)
    second = values_ref[senders:].reshape(senders * 4, 128)
    lane = lanes_of(first.shape)

    def parts_of(x):
        high = x.astype(BF16).astype(F32)
        low = x - high
        stacked = []
        for q in range(4):
            left = high if q == 0 else roll(high, 128 - 32 * q)
            right = low if q == 1 else roll(low, (160 - 32 * q) % 128)
            stacked.append(jnp.where(lane < 32, left, right))
        return jnp.concatenate(stacked, axis=0).astype(BF16)

    def forward(rows, x):
        halves = dot(fwd_high[rows], x) + dot(fwd_low[rows], x)
        return halves + roll(halves, 96)

    cosines, sines = pl.ds(0, HALF), pl.ds(HALF, HALF)
    cos_w, sin_w = forward(cosines, parts_of(first + second)), forward(sines, parts_of(first - second))
    cos_a, sin_a = spectrum_ref[cosines], spectrum_ref[sines]
    real, turned = cos_a * cos_w - sin_a * sin_w, cos_a * sin_w + sin_a * cos_w
    cos_half, sin_half = half_step[cosines], half_step[sines]
    even, odd = backward(
        inv_high, inv_low, real * cos_half + turned * sin_half, turned * cos_half - real * sin_half
    )
    count = even.shape[0]
    later = even - odd
    lane = lanes_of(later.shape)
    high = later.astype(BF16).astype(F32)
    middle = (later - high).astype(BF16).astype(F32)
    low = later - high - middle
    packed = jnp.where(lane < 32, high, jnp.where(lane < 64, roll(middle, 32), roll(low, 64))).astype(BF16)
    row = lax.broadcasted_iota(jnp.int32, (count, count), 0)
    reverse = (row + lanes_of((count, count)) == count - 1).astype(F32).astype(BF16)
    turned_round = dot(reverse, packed)
    later = turned_round + roll(turned_round, 96) + roll(turned_round, 64)
    sigma_ref[:, :count] = jnp.transpose(even + odd)[:32]
    sigma_ref[:, count:] = jnp.transpose(later)[:32]


def main_kernel(
    peers, sections,
    less_hbm, great_hbm, partner_hbm, rows_hbm, weight_hbm, source_hbm, inverse_hbm, coupling_hbm,
    fwd_high_hbm, fwd_low_hbm, inv_high_hbm, inv_low_hbm, step_hbm,
    last_fwd_high_hbm, last_fwd_low_hbm, last_inv_high_hbm, last_inv_low_hbm,
    sigma_out,
    less_ref, great_ref, partner_ref, rows_ref, weight_ref, source_ref, inverse_ref, coupling_ref,
    fwd_high, fwd_low, inv_high, inv_low, half_step,
    last_fwd_high, last_fwd_low, last_inv_high, last_inv_low, load_sem,
    values, spectrum,
    swapped, ordered, first_send, first_recv, second_send, second_recv, third_send,
    orbital_table, slab_high, slab_low, couple_high, couple_low, lift_high, lift_low,
    steps, inbox, rest, rest_in, step_high, step_low, next_send, next_recv, twin_send, twin_recv,
    upward, offset, carried, arrived, across_send, across_recv,
    send_one, recv_one, send_two, recv_two, send_three, recv_three,
):
    me = lax.axis_index("energy")
    section = lax.axis_index("section")
    has_before = section > 0
    has_after = section < sections - 1
    after = lax.rem(section + 1, sections)
    orbitals = inverse_ref.shape[0]
    half, full = orbitals // 2, orbitals // 128 * 128
    core = lax.rem(me, 2)
    in_upper = me >= peers // 2

    def as_is(place):
        return place

    def mirrored(place):
        return jnp.where(place < peers // 2, place, 3 * peers // 2 - 1 - place)

    twin = me + 1 - 2 * core

    barrier = pltpu.get_barrier_semaphore()

    def greet(n, _):
        peer = lax.rem(me + far_first(peers, n), peers)
        pl.semaphore_signal(barrier, inc=1, device_id={"energy": peer}, device_id_type=MESH)
        return 0

    lax.fori_loop(0, peers - 1, greet, 0)

    for away in range(1, REACH + 1):
        for there, other in ((section >= away, section - away), (section < sections - away, section + away)):

            @pl.when(there)
            def _(other=other):
                pl.semaphore_signal(barrier, inc=1, device_id={"section": other}, device_id_type=MESH)

    loads = [
        pltpu.make_async_copy(source, target, load_sem.at[place])
        for place, (source, target) in enumerate((
            (great_hbm, great_ref), (partner_hbm, partner_ref), (less_hbm, less_ref), (rows_hbm, rows_ref),
            (weight_hbm, weight_ref), (source_hbm, source_ref), (inverse_hbm, inverse_ref),
            (coupling_hbm, coupling_ref), (fwd_high_hbm, fwd_high), (fwd_low_hbm, fwd_low),
            (inv_high_hbm, inv_high), (inv_low_hbm, inv_low),
            (step_hbm, half_step),
            (last_fwd_high_hbm, last_fwd_high), (last_fwd_low_hbm, last_fwd_low),
            (last_inv_high_hbm, last_inv_high), (last_inv_low_hbm, last_inv_low),
        ))
    ]
    for load in loads:
        load.start()

    for load in loads[:3]:
        load.wait()

    partner = partner_ref[...]
    partner_tile, partner_lane = partner // 128, partner % 128
    for place in range(16):
        energy = pl.ds(pl.multiple_of(8 * jnp.where(in_upper, 15 - place, place), 8), 8)
        lines = great_ref[energy, :]
        total = jnp.zeros((8, 128), F32)
        for tile in range(8):
            line = jnp.broadcast_to(lines[tile : tile + 1, :], (8, 128))
            total = jnp.where(partner_tile == tile, lane_take(line, partner_lane), total)
        swapped[8 * place : 8 * place + 8, :] = total
        ordered[8 * place : 8 * place + 8, :] = less_ref[energy, :]

    for tile in range(8):
        parts = []
        for h in range(2):
            for ref in (ordered, swapped):
                parts.append(ref[pl.ds(64 * h + tile, 8, stride=8), :])
        for b, part in enumerate(exchange_groups(parts)):
            first_send[4 * tile + b] = part

    for load in loads[3:8]:
        load.wait()
    slab_high[...], slab_low[...] = split(inverse_ref[...])
    couple_high[...], couple_low[...] = split(coupling_ref[...])
    slab_map = (
        dot(slab_high[...], couple_high[...])
        + dot(slab_high[...], couple_low[...])
        + dot(slab_low[...], couple_high[...])
    )
    map_high, map_low = split(slab_map)
    index = lax.broadcasted_iota(jnp.int32, (orbitals, orbitals), 0)
    identity = (index == lanes_of((orbitals, orbitals))).astype(F32).astype(BF16)
    turned_high, turned_low = dot(identity, map_high, NT), dot(identity, map_low, NT)
    step_high[0], step_low[0] = turned_high.astype(BF16), turned_low.astype(BF16)
    turned = turned_high + turned_low
    steps[0, 0], steps[0, 1] = turned[:half], turned[half:]
    own_half = steps[0, core]
    for chunk in range(2):
        rest[0, chunk] = fold_rest(own_half[chunk_rows(chunk)])

    for away in range(1, REACH):

        @pl.when(section < away)
        def _(away=away):
            arrived[away] = jnp.zeros_like(arrived[away])

    pl.semaphore_wait(barrier, peers - 1 + jnp.minimum(section, REACH) + jnp.minimum(sections - 1 - section, REACH))
    scatter_start(peers, me, first_send, first_recv, send_one, recv_one, as_is, mirrored)

    def rows_of(chunk):
        rows = chunk_rows(chunk)
        return pl.ds(rows.start, rows.stop - rows.start)

    def to_next(k, chunk):
        def copy(source, target, place):
            return pltpu.make_async_remote_copy(
                src_ref=source,
                dst_ref=target,
                send_sem=next_send.at[k - 1, chunk, place],
                recv_sem=next_recv.at[k - 1, chunk, place],
                device_id={"section": after},
                device_id_type=MESH,
            )

        whole = pl.ds(0, full)
        return (
            copy(steps.at[k - 1, core, rows_of(chunk), whole], inbox.at[k - 1, rows_of(chunk)], 0),
            copy(rest.at[k - 1, chunk], rest_in.at[k - 1, chunk], 1),
        )

    def to_twin(k, chunk):
        return pltpu.make_async_remote_copy(
            src_ref=steps.at[k - 1, core, rows_of(chunk)],
            dst_ref=steps.at[k - 1, core, rows_of(chunk)],
            send_sem=twin_send.at[k - 1, chunk],
            recv_sem=twin_recv.at[k - 1, chunk],
            device_id={"energy": twin},
            device_id_type=MESH,
        )

    far_enough = section >= REACH

    def sends(k):
        return jnp.logical_and(has_after, section >= k) if k == REACH - 1 else has_after

    def pass_on(k, chunk):
        @pl.when(sends(k))
        def _():
            for copy in to_next(k, chunk):
                copy.start()

    def grow(k, chunk):
        @pl.when(has_before)
        def _():
            for copy in to_next(k - 1, chunk):
                copy.wait_recv()

        rows = rows_of(chunk)
        last = unfold_rest(rest_in[k - 2, chunk], rows.size)
        high, low = split(jnp.concatenate([inbox[k - 2, rows], last], axis=1))
        whole_high, whole_low = step_high[0], step_low[0]
        grown = dot(high, whole_high) + dot(low, whole_high) + dot(high, whole_low)
        steps[k - 1, core, rows] = grown
        if k < REACH:
            rest[k - 1, chunk] = fold_rest(grown)
            pass_on(k, chunk)
        to_twin(k, chunk).start()

    def gather(k):
        for chunk in range(2):
            to_twin(k, chunk).wait_recv()
        for part in range(2):
            rows = pl.ds(half * part, half)
            step_high[k - 1, rows], step_low[k - 1, rows] = split(steps[k - 1, part])

    @pl.when(jnp.logical_not(has_before))
    def _():
        inbox[...] = jnp.zeros_like(inbox)
        rest_in[...] = jnp.zeros_like(rest_in)

    for chunk in range(2):
        pass_on(1, chunk)

    pair_rows = rows_ref[...]
    for tile in range(8):
        index = lax.broadcasted_iota(jnp.int32, (orbitals, 128), 0)
        orbital_table[:, 128 * tile : 128 * tile + 128] = (
            (index == pair_rows[tile : tile + 1, :]).astype(F32).astype(BF16)
        )
    source = source_ref[...]
    base = product(jnp.broadcast_to(source, (16, orbitals)), slab_high[...], slab_low[...], NT)
    inverse_turned = dot(identity, slab_high[...], NT).astype(BF16), dot(identity, slab_low[...], NT).astype(BF16)
    lift_high[...], lift_low[...] = split(
        dot(inverse_turned[0], couple_high[...])
        + dot(inverse_turned[0], couple_low[...])
        + dot(inverse_turned[1], couple_high[...])
    )
    base_up = product(base, couple_high[...], couple_low[...], NN)
    grow(2, 0)

    for load in loads[8:13]:
        load.wait()
    wait_blocks(peers, first_recv, recv_one)

    first = first_recv[: peers // 2].reshape(peers * 4, 128)
    second = first_recv[peers // 2 :].reshape(peers * 4, 128)
    low_lanes = lanes_of(first.shape) < 64

    def parts_of(x):
        high = x.astype(BF16).astype(F32)
        low = x - high
        left = jnp.where(low_lanes, high, roll(low, 64))
        right = jnp.where(low_lanes, roll(high, 64), low)
        return jnp.concatenate([left, right], axis=0).astype(BF16)

    def forward(rows, x):
        halves = dot(fwd_high[rows], x) + dot(fwd_low[rows], x)
        return halves + roll(halves, 64)

    cosines, sines = pl.ds(0, HALF), pl.ds(HALF, HALF)
    cos_a, sin_a = forward(cosines, parts_of(first + second)), forward(sines, parts_of(first - second))
    spectrum[cosines], spectrum[sines] = cos_a, sin_a
    cos_b, sin_b = roll(cos_a, 96), roll(sin_a, 96)
    real, turned = cos_a * cos_b + sin_a * sin_b, sin_a * cos_b - cos_a * sin_b
    cos_half, sin_half = half_step[cosines], half_step[sines]
    even, odd = backward(
        inv_high, inv_low, real * cos_half - turned * sin_half, turned * cos_half + real * sin_half
    )
    group = lanes_of((peers * 2, 128)) // 32

    def join(polar):
        count = polar.shape[0] // 4
        joined = polar[:count]
        for q in range(1, 4):
            joined = jnp.where(group == q, roll(polar[count * q : count * (q + 1)], 32 * q), joined)
        return joined.reshape(peers // 2, 4, 128)

    second_send[: peers // 2] = join(even + odd)
    second_send[peers // 2 :] = join(even - odd)
    scatter_start(peers, me, second_send, second_recv, send_two, recv_two, mirrored, as_is)
    grow(2, 1)
    grow(3, 0)
    gather(2)
    wait_blocks(peers, second_recv, recv_two)

    weighted = []
    for tile in range(8):
        lines = [second_recv[4 * tile + b] for b in range(4)]
        one, two = exchange_rows(jnp.concatenate(lines[:2], axis=0), jnp.concatenate(lines[2:], axis=0))
        weighted.append(jnp.concatenate([one, two], axis=0) * weight_ref[tile : tile + 1, :])
    both = dot(jnp.concatenate(split(jnp.concatenate(weighted, axis=1)), axis=0), orbital_table[...], NT)
    local_pol = both[:16] + both[16:]
    spread = local_pol * base
    upward[...] = base_up + product(spread, lift_high[...], lift_low[...], NN)

    def across(source, place, away):
        return pltpu.make_async_remote_copy(
            src_ref=source,
            dst_ref=arrived.at[place],
            send_sem=across_send.at[place],
            recv_sem=across_recv.at[place],
            device_id={"section": lax.rem(section + sections + away, sections)},
            device_id_type=MESH,
        )

    shift = across(upward, 0, -1)
    window = [across(offset, away, away) for away in range(1, REACH)]
    sweep = across(carried, REACH, REACH)

    @pl.when(has_before)
    def _():
        shift.start()

    grow(3, 1)
    guess = base + product(spread, slab_high[...], slab_low[...], NT)
    partial = product(source + local_pol * guess, slab_high[...], slab_low[...], NT)
    gather(3)

    @pl.when(far_enough)
    def _():
        grow(4, 0)


    @pl.when(has_after)
    def _():
        shift.wait_recv()

    @pl.when(jnp.logical_not(has_after))
    def _():
        arrived[0] = jnp.zeros_like(upward)

    offset[...] = partial + product(arrived[0], slab_high[...], slab_low[...], NT)
    for away in range(1, REACH):

        @pl.when(section < sections - away)
        def _(away=away):
            window[away - 1].start()


    @pl.when(far_enough)
    def _():
        grow(4, 1)
        gather(4)

    so_far = offset[...]
    for away in range(1, REACH):

        @pl.when(section >= away)
        def _(away=away):
            window[away - 1].wait_recv()

        if away != 2:
            for near in (1,) if away == 1 else (2, 3):
                so_far += product(arrived[near], step_high[near - 1], step_low[near - 1], NN)
    carried[...] = so_far

    @pl.when(section < REACH)
    def _():
        sweep.start()


    @pl.when(section >= REACH)
    def _():
        sweep.wait_recv()
        carried[...] += product(arrived[REACH], step_high[REACH - 1], step_low[REACH - 1], NN)

        @pl.when(section < sections - REACH)
        def _():
            sweep.start()

    screened = carried[...]
    both = dot(jnp.concatenate(split(screened), axis=0), orbital_table[...])
    pairs = both[:16] + both[16:]
    for tile in range(8):
        piece = pairs[:, 128 * tile : 128 * tile + 128] * weight_ref[tile : tile + 1, :]
        one, two = exchange_rows(piece[:8], piece[8:])
        for b, block in enumerate((one[:4], one[4:], two[:4], two[4:])):
            third_send[4 * tile + b] = block
    scatter_start(peers, me, third_send, values, send_three, recv_three, as_is, mirrored)

    for load in loads[13:]:
        load.wait()
    wait_blocks(peers, values, recv_three)
    convolve(
        values, spectrum, last_fwd_high, last_fwd_low, last_inv_high, last_inv_low, half_step, sigma_out
    )

    @pl.when(has_before)
    def _():
        shift.wait_send()

    for away in range(1, REACH):

        @pl.when(section < sections - away)
        def _(away=away):
            window[away - 1].wait_send()

    @pl.when(section < sections - REACH)
    def _():
        sweep.wait_send()

    for chunk in range(2):

        for k in range(1, REACH):

            @pl.when(sends(k))
            def _(k=k, chunk=chunk):
                for copy in to_next(k, chunk):
                    copy.wait_send()

        for k in range(2, REACH):
            to_twin(k, chunk).wait_send()

        @pl.when(far_enough)
        def _(chunk=chunk):
            to_twin(REACH, chunk).wait_send()

    wait_blocks(peers, first_send, send_one)
    wait_blocks(peers, second_send, send_two)
    wait_blocks(peers, third_send, send_three)


def on_device(peers, sections, g_less, g_greater, partner, pair_rows, pair_weight, source, slab_inverse, coupling):
    own, _, columns = g_less.shape
    energies = own * peers
    orbitals = slab_inverse.shape[-1]
    vmem = pl.BlockSpec(memory_space=pltpu.VMEM)
    hbm = pl.BlockSpec(memory_space=pltpu.HBM)
    square = (orbitals, orbitals)
    strip = (own, orbitals)
    sigma = pl.pallas_call(
        functools.partial(main_kernel, peers, sections),
        out_shape=pltpu.VMEM((columns // peers, energies), F32),
        in_specs=[hbm] * 17,
        out_specs=vmem,
        scratch_shapes=[
            pltpu.VMEM((128, 128), F32),
            pltpu.VMEM((128, 128), F32),
            pltpu.VMEM((8, 128), jnp.int32),
            pltpu.VMEM((8, 128), jnp.int32),
            pltpu.VMEM((8, 128), F32),
            pltpu.VMEM((1, orbitals), F32),
            pltpu.VMEM(square, F32),
            pltpu.VMEM(square, F32),
            pltpu.VMEM((LENGTH, energies // 2), BF16),
            pltpu.VMEM((LENGTH, energies // 2), BF16),
            pltpu.VMEM((energies, HALF), BF16),
            pltpu.VMEM((energies, HALF), BF16),
            pltpu.VMEM((LENGTH, 128), F32),
            pltpu.VMEM((LENGTH, energies // 2), BF16),
            pltpu.VMEM((LENGTH, energies // 2), BF16),
            pltpu.VMEM((energies, HALF), BF16),
            pltpu.VMEM((energies, HALF), BF16),
            pltpu.SemaphoreType.DMA((17,)),
            pltpu.VMEM((peers, 4, 128), F32),
            pltpu.VMEM((LENGTH, 128), F32),
            pltpu.VMEM((128, 128), F32),
            pltpu.VMEM((128, 128), F32),
            pltpu.VMEM((peers, 8, 128), F32),
            pltpu.VMEM((peers, 8, 128), F32),
            pltpu.VMEM((peers, 4, 128), F32),
            pltpu.VMEM((peers, 4, 128), F32),
            pltpu.VMEM((peers, 4, 128), F32),
            pltpu.VMEM((orbitals, columns), BF16),
            pltpu.VMEM(square, BF16),
            pltpu.VMEM(square, BF16),
            pltpu.VMEM(square, BF16),
            pltpu.VMEM(square, BF16),
            pltpu.VMEM(square, BF16),
            pltpu.VMEM(square, BF16),
            pltpu.VMEM((REACH, 2, orbitals // 2, orbitals), F32),
            pltpu.VMEM((REACH - 1, orbitals // 2, orbitals // 128 * 128), F32),
            pltpu.VMEM((REACH - 1, 2, 32, 128), F32),
            pltpu.VMEM((REACH - 1, 2, 32, 128), F32),
            pltpu.VMEM((REACH,) + square, BF16),
            pltpu.VMEM((REACH,) + square, BF16),
            pltpu.SemaphoreType.DMA((REACH, 2, 2)),
            pltpu.SemaphoreType.DMA((REACH, 2, 2)),
            pltpu.SemaphoreType.DMA((REACH, 2)),
            pltpu.SemaphoreType.DMA((REACH, 2)),
            pltpu.VMEM(strip, F32),
            pltpu.VMEM(strip, F32),
            pltpu.VMEM(strip, F32),
            pltpu.VMEM((REACH + 1,) + strip, F32),
            pltpu.SemaphoreType.DMA((REACH + 1,)),
            pltpu.SemaphoreType.DMA((REACH + 1,)),
        ]
        + [pltpu.SemaphoreType.DMA] * 6,
        compiler_params=pltpu.CompilerParams(
            collective_id=0, has_side_effects=True, vmem_limit_bytes=60 * 1024 * 1024
        ),
        name="update",
    )(
        g_less.reshape(-1, 128),
        g_greater.reshape(-1, 128),
        partner.reshape(-1, 128),
        pair_rows.reshape(-1, 128),
        pair_weight.reshape(-1, 128),
        source,
        slab_inverse[0],
        coupling[0],
        *forward_table(energy_order(peers, own, 2), energies),
        *inverse_table(energy_order(peers, own, 4), energies),
        half_steps(),
        *forward_table(energy_order(peers, own, 4), energies),
        *inverse_table(np.arange(energies // 2), energies),
    )
    return jnp.transpose(sigma)[:, None, :]


def solution(mesh):
    return jax.shard_map(
        functools.partial(on_device, mesh.shape["energy"], mesh.shape["section"]),
        mesh=mesh,
        in_specs=(
            P("energy", "section", None),
            P("energy", "section", None),
            P("section", None),
            P("section", None),
            P("section", None),
            P("section", None),
            P("section", None, None),
            P("section", None, None),
        ),
        out_specs=P(None, "section", "energy"),
        check_vma=False,
    )
```
